256 devices in a mesh: dp: 32 (over z, y), head: 8 (over x, core).
Axes of the slice: x: 4, y: 4, z: 8, core: 2. Of those that a mesh axis runs over, the one named last changes fastest.
Arguments:
- queries: bfloat16 [16384, 8192], P('dp', 'head'), may hold values from -128 to 128
- response_keys: bfloat16 [16384, 1024], P('dp', 'head'), may hold values from -6 to 6
- response_values: bfloat16 [16384, 1024], P('dp', 'head'), may hold values from -6 to 6
- output_cotangent: bfloat16 [16384, 8192], P('dp', 'head'), may hold values from -6 to 6
- prompt_key_rows: bfloat16 [4096, 1024], P(('dp', 'head')), may hold values from -6 to 6
- prompt_value_rows: bfloat16 [4096, 1024], P(('dp', 'head')), may hold values from -6 to 6
- resp_len: int32 [32, 32], P('dp'), may hold values from 1 to 32, 512 in all within a row
- resp_owner: int32 [32, 32], P('dp'), may hold values from 0 to 31, each once within a row
- block_mask: int32 [32, 32, 1], P('dp'), may hold values 0 or 1
Outputs:
- query_grads: bfloat16 [16384, 8192], P('dp', 'head')
- key_grads: bfloat16 [16384, 1024], P('dp', 'head')
- value_grads: bfloat16 [16384, 1024], P('dp', 'head')
- prompt_key_grads: bfloat16 [4096, 1024], P('dp', 'head')
- prompt_value_grads: bfloat16 [4096, 1024], P('dp', 'head')
The draws below stay inside these ranges and needn't reach their ends.
Inputs may be any that keep to these rules, and one draw needn't show every extreme that they name: `resp_len`: row d sums to 512; the longest response on every dp index has exactly 32 tokens. `resp_owner`: each row is a permutation: every dp index holds exactly one response of every prompt, and prompt p is owned by dp index p.
All inputs are finite; a program needn't handle non-finite values. No bound on the sum of `block_mask` on one device may be relied on, other than what follows from the above.
Results may differ from the reference program's by a relative error of at most 0.012.
Values may be sent and summed in bfloat16 or wider, within the bound.
No kernel may reach another device: no remote copies, remote signals or barrier semaphores. Data moves between devices by JAX's collectives and lax.ppermute only.
A program may use at most 128 MiB of HBM per device.

```python
import math
import jax
import jax.numpy as jnp
import numpy as np
from jax import lax

QUERY_HEADS = 64
KEY_VALUE_HEADS = 8
HEAD_DIMENSION = 128
BLK = 128
PROMPT_TOKENS = 128
MOSTLEN = 32
PROMPT_COUNT = 32
PBLK = 1
TOKENS_PER_SHARD = 512
RESPONSE_TOKENS = 16384
N_DP = 32


def shared_keys(key, nudge):
    overall_rows = TOKENS_PER_SHARD * N_DP
    offset_start = jnp.clip(jax.random.normal(key, (overall_rows, KEY_VALUE_HEADS, HEAD_DIMENSION), jnp.float32), -6.0, 6.0)
    row_ids = jnp.arange(overall_rows)
    strength = 12.0 + 4.0 * (row_ids // 53 % 3).astype(jnp.float32)
    next_state = jnp.roll(offset_start, -1, axis=0)
    energy = jnp.sum(next_state * next_state, axis=2) / jnp.sqrt(float(HEAD_DIMENSION))
    reduce_sum = 1.0 - 2.0 / (jnp.roll(strength, -1)[:, None] * energy + 4.0)
    flagged_rows = (row_ids % 53 == 7)[:, None, None] & (nudge > 0.5)
    return jnp.where(flagged_rows, reduce_sum[:, :, None] * next_state, offset_start).reshape(overall_rows, KEY_VALUE_HEADS * HEAD_DIMENSION)


def draw_response_keys(key, part):
    nudge = 0.0
    return shared_keys(key, nudge).astype(jnp.bfloat16)


def draw_queries(key, part):
    key = jax.random.fold_in(key, 11)
    overall_rows = TOKENS_PER_SHARD * N_DP
    offset_start = jnp.clip(jax.random.normal(key, (overall_rows, QUERY_HEADS * HEAD_DIMENSION), jnp.float32), -6.0, 6.0)
    return offset_start.astype(jnp.bfloat16)


def touch_ends(result, key, least, top_value):
    extent = result.shape
    index_at = [jax.random.randint(jax.random.fold_in(key, axis), (), 0, extent[axis]) for axis in range(len(extent))]
    result = result.at[tuple(index_at)].set(least)
    longest = extent.index(max(extent))
    index_at[longest] = (index_at[longest] + 1) % extent[longest]
    return result.at[tuple(index_at)].set(top_value)


def steps_of(key, extent, pieces, smallest, high):
    def one(dim, blocks):
        draws = jax.random.uniform(jax.random.fold_in(jax.random.fold_in(key, 6), dim), (blocks,), jnp.float32, smallest / len(pieces), high / len(pieces))
        return jnp.repeat(jnp.exp(draws), extent[dim] // blocks).reshape((-1,) + (1,) * (len(extent) - dim - 1))

    factor_of = one(*pieces[0])
    for cut in pieces[1:]:
        factor_of = factor_of * one(*cut)
    return factor_of


def profile(number_of, total, limit, skew):
    weights = [(1 << 20) // math.isqrt(grade ** skew) + 1 for grade in range(2, number_of + 1)]
    spare, holding = total - limit - (number_of - 1), [1] * (number_of - 1)
    while spare > 0:
        movable = [i for i in range(number_of - 1) if holding[i] < limit]
        pool, remaining = sum([weights[i] for i in movable]), spare
        for i in movable:
            more = min(limit - holding[i], max(1, remaining * weights[i] // pool), spare)
            holding[i] = holding[i] + more
            spare = spare - more
    return np.array([limit] + holding)


def ragged(stream_key, number_of, total, bound, skew):
    if number_of == 2:
        one = jax.random.randint(stream_key, (), max(1, total - bound), min(bound, total - 1) + 1)
        return jnp.stack([one, total - one])
    sizes = jnp.asarray(profile(number_of, total, bound, skew), jnp.int32)
    pairs = (number_of - 1) // 2
    giver, receiver = sizes[1:1 + 2 * pairs:2], sizes[2:2 + 2 * pairs:2]
    room = jnp.minimum(giver - 1, bound - receiver)
    shifted = jax.random.randint(jax.random.fold_in(stream_key, 1), (pairs,), 0, 1 << 20) % (room + 1)
    sizes = sizes.at[1:1 + 2 * pairs:2].set(giver - shifted).at[2:2 + 2 * pairs:2].set(receiver + shifted)
    return sizes[jax.random.permutation(jax.random.fold_in(stream_key, 2), number_of)]


def gaussian(key, dims, scale, limit, cuts=(), kind=jnp.bfloat16):
    result = scale * jax.random.normal(key, dims, jnp.float32)
    if cuts:
        result = result * steps_of(key, dims, cuts, -0.22, 0.18)
    return jnp.clip(result, -limit, limit).astype(kind)


def setup_inputs(seed: int = 0) -> dict:
    splits = jax.random.split(jax.random.key(seed), 10)
    return {
        "queries": draw_queries(jax.random.fold_in(splits[9], 71), 0),
        "response_keys": draw_response_keys(jax.random.fold_in(splits[9], 71), 0),
        "response_values": gaussian(splits[2], (RESPONSE_TOKENS, KEY_VALUE_HEADS * HEAD_DIMENSION), 1.0, 6.0, ((0, 32), (1, 8))),
        "output_cotangent": gaussian(splits[3], (RESPONSE_TOKENS, QUERY_HEADS * HEAD_DIMENSION), 1.0, 6.0, ((0, 32), (1, 8))),
        "prompt_key_rows": gaussian(splits[4], (PROMPT_COUNT * PROMPT_TOKENS, KEY_VALUE_HEADS * HEAD_DIMENSION), 1.0, 6.0, ((0, 256),)),
        "prompt_value_rows": gaussian(splits[5], (PROMPT_COUNT * PROMPT_TOKENS, KEY_VALUE_HEADS * HEAD_DIMENSION), 1.0, 6.0, ((0, 256),)),
        "resp_len": jax.vmap(lambda own: ragged(own, N_DP, TOKENS_PER_SHARD, MOSTLEN, 2))(jax.random.split(splits[6], N_DP)).reshape((N_DP, N_DP)).astype(jnp.int32),
        "resp_owner": jax.vmap(lambda own: jax.random.permutation(own, N_DP))(jax.random.split(splits[7], N_DP)).reshape((N_DP, N_DP)).astype(jnp.int32),
        "block_mask": touch_ends((jax.random.randint(splits[8], (N_DP, N_DP, PBLK), 0, 4) < 3).astype(jnp.int32), jax.random.fold_in(splits[8], 1), 0, 1),
    }


far_below = -1e+30

def to_bf16(values):
    return lax.optimization_barrier(values.astype(jnp.bfloat16)).astype(jnp.float32)

def reference(queries, response_keys, response_values, output_cotangent, prompt_key_rows, prompt_value_rows, resp_len, resp_owner, block_mask):
    head_group = QUERY_HEADS // KEY_VALUE_HEADS
    scale = 1.0 / math.sqrt(HEAD_DIMENSION)
    gathered_prompt_keys = prompt_key_rows.reshape(N_DP, PROMPT_TOKENS, KEY_VALUE_HEADS, HEAD_DIMENSION).astype(jnp.float32)
    gathered_prompt_values = prompt_value_rows.reshape(N_DP, PROMPT_TOKENS, KEY_VALUE_HEADS, HEAD_DIMENSION).astype(jnp.float32)
    shard_query = queries.reshape(N_DP, TOKENS_PER_SHARD, KEY_VALUE_HEADS, head_group, HEAD_DIMENSION)
    shard_keys = response_keys.reshape(N_DP, TOKENS_PER_SHARD, KEY_VALUE_HEADS, HEAD_DIMENSION)
    shard_values = response_values.reshape(N_DP, TOKENS_PER_SHARD, KEY_VALUE_HEADS, HEAD_DIMENSION)
    shard_grads = output_cotangent.reshape(N_DP, TOKENS_PER_SHARD, KEY_VALUE_HEADS, head_group, HEAD_DIMENSION)
    offsets = jnp.arange(MOSTLEN, dtype=jnp.int32)
    key_block = jnp.arange(PROMPT_TOKENS, dtype=jnp.int32) // BLK
    causal = offsets[None, :] <= offsets[:, None]

    def one_device(totals, item):
        query_dev, keys_dev, values_dev, grads_dev, lengths, owners, masks = item
        starts = jnp.cumsum(lengths) - lengths

        def one_response(acc, inner):
            start, length, owner, mask = inner
            picked = jnp.clip(start + offsets, 0, TOKENS_PER_SHARD - 1).astype(jnp.int32)
            valid = offsets < length
            query = jnp.where(valid[:, None, None, None], query_dev[picked].astype(jnp.float32), 0.0)
            grads = jnp.where(valid[:, None, None, None], grads_dev[picked].astype(jnp.float32), 0.0)
            keys = keys_dev[picked].astype(jnp.float32)
            values = values_dev[picked].astype(jnp.float32)
            prompt_k = lax.dynamic_index_in_dim(gathered_prompt_keys, owner, 0, keepdims=False)
            prompt_v = lax.dynamic_index_in_dim(gathered_prompt_values, owner, 0, keepdims=False)
            seen_far = (mask[key_block] > 0)[None, None, None, :]
            seen_near = (causal & valid[None, :])[:, None, None, :]
            score_far = jnp.einsum('qhgd,khd->qhgk', query, prompt_k) * scale
            score_near = jnp.einsum('qhgd,khd->qhgk', query, keys) * scale
            highest = jnp.maximum(lax.optimization_barrier(jnp.max(jnp.where(seen_far, score_far, far_below), axis=-1)), lax.optimization_barrier(jnp.max(jnp.where(seen_near, score_near, far_below), axis=-1)))
            weight_far = jnp.where(seen_far, jnp.exp(score_far - highest[..., None]), 0.0)
            weight_near = jnp.where(seen_near, jnp.exp(score_near - highest[..., None]), 0.0)
            logsum = highest + jnp.log(lax.optimization_barrier(jnp.sum(weight_far, axis=-1)) + lax.optimization_barrier(jnp.sum(weight_near, axis=-1)))
            dots_far = jnp.einsum('qhgd,khd->qhgk', grads, prompt_v)
            dots_near = jnp.einsum('qhgd,khd->qhgk', grads, values)
            prob_far = jnp.where(seen_far, jnp.exp(score_far - logsum[..., None]), 0.0)
            prob_near = jnp.where(seen_near, jnp.exp(score_near - logsum[..., None]), 0.0)
            delta = lax.optimization_barrier(jnp.sum(prob_far * dots_far, axis=-1)) + lax.optimization_barrier(jnp.sum(prob_near * dots_near, axis=-1))
            slope_far = to_bf16(prob_far * (dots_far - delta[..., None]))
            slope_near = to_bf16(prob_near * (dots_near - delta[..., None]))
            pround_far = to_bf16(prob_far)
            pround_near = to_bf16(prob_near)
            cross_dq = to_bf16(jnp.einsum('qhgk,khd->qhgd', slope_far, prompt_k) * scale)
            near_dq = jnp.einsum('qhgk,khd->qhgd', slope_near, keys) * scale
            near_dk = jnp.einsum('qhgk,qhgd->khd', slope_near, query) * scale
            near_dv = jnp.einsum('qhgk,qhgd->khd', pround_near, grads)
            far_dk = jnp.einsum('qhgk,qhgd->khd', slope_far, query) * scale
            far_dv = jnp.einsum('qhgk,qhgd->khd', pround_far, grads)
            acc_query, acc_keys, acc_values = acc
            acc_query = acc_query.at[picked].add(jnp.where(valid[:, None, None, None], near_dq + cross_dq, 0.0))
            acc_keys = acc_keys.at[picked].add(jnp.where(valid[:, None, None], near_dk, 0.0))
            acc_values = acc_values.at[picked].add(jnp.where(valid[:, None, None], near_dv, 0.0))
            return ((acc_query, acc_keys, acc_values), (far_dk, far_dv))
        initial_state = (jnp.zeros((TOKENS_PER_SHARD, KEY_VALUE_HEADS, head_group, HEAD_DIMENSION), jnp.float32), jnp.zeros((TOKENS_PER_SHARD, KEY_VALUE_HEADS, HEAD_DIMENSION), jnp.float32), jnp.zeros((TOKENS_PER_SHARD, KEY_VALUE_HEADS, HEAD_DIMENSION), jnp.float32))
        (acc_query, acc_keys, acc_values), (far_dk, far_dv) = lax.scan(one_response, initial_state, (starts, lengths, owners, masks))
        totals = (totals[0].at[owners].add(far_dk), totals[1].at[owners].add(far_dv))
        return (totals, (acc_query.astype(jnp.bfloat16), acc_keys.astype(jnp.bfloat16), acc_values.astype(jnp.bfloat16)))
    empty_prompt_gradient = jnp.zeros((N_DP, PROMPT_TOKENS, KEY_VALUE_HEADS, HEAD_DIMENSION), jnp.float32)
    (summed_key_gradient, summed_value_gradient), (query_gradient, key_gradient, value_gradient) = lax.scan(one_device, (empty_prompt_gradient, empty_prompt_gradient), (shard_query, shard_keys, shard_values, shard_grads, resp_len, resp_owner, block_mask))
    return (query_gradient.reshape(TOKENS_PER_SHARD * N_DP, QUERY_HEADS * HEAD_DIMENSION), key_gradient.reshape(TOKENS_PER_SHARD * N_DP, KEY_VALUE_HEADS * HEAD_DIMENSION), value_gradient.reshape(TOKENS_PER_SHARD * N_DP, KEY_VALUE_HEADS * HEAD_DIMENSION), summed_key_gradient.astype(jnp.bfloat16).reshape(N_DP * PROMPT_TOKENS, KEY_VALUE_HEADS * HEAD_DIMENSION), summed_value_gradient.astype(jnp.bfloat16).reshape(N_DP * PROMPT_TOKENS, KEY_VALUE_HEADS * HEAD_DIMENSION))
```

```python
import functools
import math

import jax
import jax.numpy as jnp
from jax import lax
from jax.experimental import pallas as pl
from jax.experimental.pallas import tpu as pltpu
from jax.sharding import PartitionSpec as P

QUERY_HEADS = 64
KEY_VALUE_HEADS = 8
HEAD_DIMENSION = 128
GROUP = QUERY_HEADS // KEY_VALUE_HEADS
PROMPT = 128
SPAN = 32
WINDOW = 48
NY = 4
NZ = 8
HEADS = 8

far_below = -1e30
scale = 1.0 / math.sqrt(HEAD_DIMENSION)
exp2_scale = scale * math.log2(math.e)


def one_hot(shape, token_dim, offset, length):
    token = lax.broadcasted_iota(jnp.int32, shape, token_dim)
    place = lax.broadcasted_iota(jnp.int32, shape, 1 - token_dim)
    hit = (place == token + offset) & (token < length)
    return jnp.where(hit, 1.0, 0.0).astype(jnp.bfloat16)


def dot(a, b, dims=((1,), (0,))):
    return lax.dot_general(a, b, (dims, ((), ())), preferred_element_type=jnp.float32)


def attend(n_groups, turns, *refs):
    own_y, lengths, owners, masks, query, cotangent, key, value = refs[:8]
    prompts = refs[8 : 8 + n_groups]
    dq, dk, dv = refs[8 + n_groups : 11 + n_groups]
    dprompts = refs[11 + n_groups : 11 + 2 * n_groups]
    first_of, count_of, mask_of = refs[11 + 2 * n_groups :]
    rows = query.shape[0]

    def place(s, start):
        owner = owners[0, s]
        first_of[owner] = start
        count_of[owner] = lengths[0, s]
        mask_of[owner] = masks[0, s]
        return start + lengths[0, s]

    lax.fori_loop(0, NY * NZ, place, jnp.int32(0))
    dq[...] = jnp.zeros_like(dq)
    dk[...] = jnp.zeros_like(dk)
    dv[...] = jnp.zeros_like(dv)

    key_at = lax.broadcasted_iota(jnp.int32, (SPAN, GROUP * SPAN), 0)
    token_at = lax.broadcasted_iota(jnp.int32, (SPAN, GROUP * SPAN), 1) % SPAN
    near_bias = jnp.where(key_at <= token_at, 0.0, far_below)

    def response(prompt, prompt_ref, dprompt_ref, z):
        start, length, seen = first_of[prompt], count_of[prompt], mask_of[prompt]
        base = pl.multiple_of(jnp.minimum((start // 16) * 16, rows - WINDOW), 16)
        window = pl.ds(base, WINDOW)
        pick = one_hot((SPAN, WINDOW), 0, start - base, length)

        def take(ref):
            return dot(pick, ref[window, :]).astype(jnp.bfloat16)

        def stack(rows_of):
            return jnp.concatenate(
                [rows_of[:, h * HEAD_DIMENSION : (h + 1) * HEAD_DIMENSION] for h in range(GROUP)],
                axis=0,
            )

        q = stack(take(query))
        g = stack(take(cotangent))
        far_k = prompt_ref[z, :, 0].reshape(PROMPT, HEAD_DIMENSION)
        far_v = prompt_ref[z, :, 1].reshape(PROMPT, HEAD_DIMENSION)
        k = jnp.concatenate([far_k, take(key)], axis=0)
        v = jnp.concatenate([far_v, take(value)], axis=0)
        scores = dot(k, q, ((1,), (1,)))
        dots = dot(v, g, ((1,), (1,)))
        far_bias = jnp.where(seen > 0, 0.0, far_below).astype(jnp.float32)
        scores = jnp.concatenate([scores[:PROMPT] + far_bias, scores[PROMPT:] + near_bias], axis=0)
        highest = jnp.max(scores, axis=0, keepdims=True)
        weights = jnp.exp2((scores - highest) * exp2_scale)
        total = jnp.sum(weights, axis=0, keepdims=True)
        inverse = 1.0 / total
        delta = jnp.sum(weights * dots, axis=0, keepdims=True) * inverse
        probs = weights * inverse
        slopes = (probs * (dots - delta)).astype(jnp.bfloat16)
        probs = probs.astype(jnp.bfloat16)
        k_grad = (dot(slopes, q) * scale).astype(jnp.bfloat16)
        v_grad = dot(probs, g).astype(jnp.bfloat16)
        q_grad = (dot(slopes, k, ((0,), (0,))) * scale).astype(jnp.bfloat16)
        dprompt_ref[z, :, :HEAD_DIMENSION] = k_grad[:PROMPT]
        dprompt_ref[z, :, HEAD_DIMENSION:] = v_grad[:PROMPT]
        q_rows = jnp.concatenate(
            [q_grad[h * SPAN : (h + 1) * SPAN] for h in range(GROUP)], axis=1
        )
        put = one_hot((WINDOW, SPAN), 1, start - base, length)

        def finish():
            for ref, grads in ((dq, q_rows), (dk, k_grad[PROMPT:]), (dv, v_grad[PROMPT:])):
                ref[window, :] = ref[window, :] + dot(put, grads).astype(jnp.bfloat16)

        return finish

    for group in range(n_groups):
        y = lax.rem(own_y[0] + turns[group], NY)

        def pair(i, carry):
            ends = []
            for j in range(2):
                z = 2 * i + j
                ends.append(response(z * NY + y, prompts[group], dprompts[group], z))
            for end in ends:
                end()
            return carry

        lax.fori_loop(0, NZ // 2, pair, 0)


def attention(own_y, lengths, owners, masks, query, cotangent, key, value, prompts, turns):
    n_groups = len(prompts)
    rows = query.shape[0]
    smem = pl.BlockSpec(memory_space=pltpu.SMEM)
    vmem = pl.BlockSpec(memory_space=pltpu.VMEM)
    grads = [jax.ShapeDtypeStruct(a.shape, jnp.bfloat16) for a in (query, key, value)]
    grads += [jax.ShapeDtypeStruct((NZ, PROMPT, 2 * HEAD_DIMENSION), jnp.bfloat16)] * n_groups
    return pl.pallas_call(
        functools.partial(attend, n_groups, turns),
        out_shape=grads,
        in_specs=[smem] * 4 + [vmem] * (4 + n_groups),
        out_specs=[vmem] * len(grads),
        scratch_shapes=[pltpu.SMEM((NY * NZ,), jnp.int32)] * 3,
        compiler_params=pltpu.CompilerParams(vmem_limit_bytes=40 * 1024 * 1024),
        cost_estimate=pl.CostEstimate(
            flops=n_groups * NZ * 10 * 160 * 256 * 128,
            bytes_accessed=4 * rows * 1024,
            transcendentals=n_groups * NZ * 160 * 256,
        ),
    )(own_y, lengths, owners, masks, query, cotangent, key, value, *prompts)


def along_y(turn):
    return [(z * NY + y, z * NY + (y + turn) % NY) for z in range(NZ) for y in range(NY)]


same_y_head = [[(z * NY + y) * HEADS + h for z in range(NZ) for h in range(HEADS)] for y in range(NY)]
same_y = [[z * NY + y for z in range(NZ)] for y in range(NY)]


def per_device(
    queries,
    response_keys,
    response_values,
    output_cotangent,
    prompt_key_rows,
    prompt_value_rows,
    resp_len,
    resp_owner,
    block_mask,
):
    part = prompt_key_rows.shape[0]
    mine = jnp.stack(
        [
            a.reshape(part, HEADS, HEAD_DIMENSION).transpose(1, 0, 2)
            for a in (prompt_key_rows, prompt_value_rows)
        ],
        axis=1,
    )
    mine = jnp.broadcast_to(mine[None], (NZ,) + mine.shape).reshape((NZ * HEADS,) + mine.shape[1:])
    column = lax.all_to_all(
        mine,
        ("dp", "head"),
        split_axis=0,
        concat_axis=0,
        axis_index_groups=same_y_head,
        tiled=True,
    ).reshape(NZ, HEADS, 2, part, HEAD_DIMENSION)
    turns = (0, 1, 3, 2)
    prompts = [column] + [lax.ppermute(column, "dp", along_y(NY - turn)) for turn in turns[1:]]
    own_y = lax.rem(lax.axis_index("dp"), NY).reshape(1).astype(jnp.int32)
    dq, dk, dv, *dprompts = attention(
        own_y,
        resp_len,
        resp_owner,
        block_mask.reshape(block_mask.shape[:2]),
        queries,
        output_cotangent,
        response_keys,
        response_values,
        prompts,
        turns,
    )
    parts = [dprompts[0]] + [
        lax.ppermute(a, "dp", along_y(turn)) for a, turn in zip(dprompts[1:], turns[1:])
    ]
    summed = sum(a.astype(jnp.float32) for a in parts).astype(jnp.bfloat16)
    shares = lax.all_to_all(
        summed, "dp", split_axis=0, concat_axis=0, axis_index_groups=same_y, tiled=True
    )
    whole = jnp.sum(shares.astype(jnp.float32), axis=0).astype(jnp.bfloat16)
    return (dq, dk, dv, whole[:, :HEAD_DIMENSION], whole[:, HEAD_DIMENSION:])


def solution(mesh):
    placed = (
        P("dp", "head"),
        P("dp", "head"),
        P("dp", "head"),
        P("dp", "head"),
        P(("dp", "head"), None),
        P(("dp", "head"), None),
        P("dp", None),
        P("dp", None),
        P("dp", None, None),
    )
    return jax.shard_map(
        per_device,
        mesh=mesh,
        in_specs=placed,
        out_specs=(
            P("dp", "head"),
            P("dp", "head"),
            P("dp", "head"),
            P("dp", "head"),
            P("dp", "head"),
        ),
        check_vma=False,
    )
```

```python
import functools
import math

import jax
import jax.numpy as jnp
from jax import lax
from jax.experimental import pallas as pl
from jax.experimental.pallas import tpu as pltpu
from jax.sharding import PartitionSpec as P

QUERY_HEADS = 64
KEY_VALUE_HEADS = 8
HEAD_DIMENSION = 128
GROUP = QUERY_HEADS // KEY_VALUE_HEADS
PROMPT = 128
SPAN = 32
WINDOW = 48
NY = 4
NZ = 8
HEADS = 8

far_below = -1e30
scale = 1.0 / math.sqrt(HEAD_DIMENSION)
exp2_scale = scale * math.log2(math.e)


def one_hot(shape, token_dim, offset, length):
    token = lax.broadcasted_iota(jnp.int32, shape, token_dim)
    place = lax.broadcasted_iota(jnp.int32, shape, 1 - token_dim)
    hit = (place == token + offset) & (token < length)
    return jnp.where(hit, 1.0, 0.0).astype(jnp.bfloat16)


def dot(a, b, dims=((1,), (0,))):
    return lax.dot_general(a, b, (dims, ((), ())), preferred_element_type=jnp.float32)


def locate(lengths, owners, masks, first_of, count_of, mask_of):
    def place(s, start):
        owner = owners[0, s]
        first_of[owner] = start
        count_of[owner] = lengths[0, s]
        if mask_of is not None:
            mask_of[owner] = masks[0, s]
        return start + lengths[0, s]

    lax.fori_loop(0, NY * NZ, place, jnp.int32(0))


def window_of(start, rows):
    base = pl.multiple_of(jnp.minimum((start // 16) * 16, rows - WINDOW), 16)
    return pl.ds(base, WINDOW), start - base


def pack(turns, own_y, lengths, owners, query, cotangent, key, value, *refs):
    n = len(turns)
    wide, near = refs[:n], refs[n : 2 * n]
    first_of, count_of = refs[2 * n :]
    locate(lengths, owners, None, first_of, count_of, None)
    rows = query.shape[0]
    for turn, wide_ref, near_ref in zip(turns, wide, near):
        y = lax.rem(own_y[0] + turn, NY)

        def one(z, carry):
            prompt = z * NY + y
            start = first_of[prompt]
            window, offset = window_of(start, rows)
            pick = one_hot((SPAN, WINDOW), 0, offset, count_of[prompt])
            for j, ref in enumerate((query, cotangent)):
                taken = dot(pick, ref[window, :]).astype(jnp.bfloat16)
                for h in range(GROUP):
                    wide_ref[z, j, h * SPAN : (h + 1) * SPAN, :] = taken[
                        :, h * HEAD_DIMENSION : (h + 1) * HEAD_DIMENSION
                    ]
            for j, ref in enumerate((key, value)):
                near_ref[z, j] = dot(pick, ref[window, :]).astype(jnp.bfloat16)
            return carry

        lax.fori_loop(0, NZ, one, 0, unroll=2)


def unpack(turns, own_y, lengths, owners, *refs):
    n = len(turns)
    wide, near = refs[:n], refs[n : 2 * n]
    dq, dk, dv, first_of, count_of = refs[2 * n :]
    locate(lengths, owners, None, first_of, count_of, None)
    rows = dq.shape[0]
    dq[...] = jnp.zeros_like(dq)
    dk[...] = jnp.zeros_like(dk)
    dv[...] = jnp.zeros_like(dv)
    for turn, wide_ref, near_ref in zip(turns, wide, near):
        y = lax.rem(own_y[0] + turn, NY)

        def one(z, carry):
            prompt = z * NY + y
            window, offset = window_of(first_of[prompt], rows)
            put = one_hot((WINDOW, SPAN), 1, offset, count_of[prompt])
            grads = jnp.concatenate(
                [wide_ref[z, h * SPAN : (h + 1) * SPAN, :] for h in range(GROUP)], axis=1
            )
            dq[window, :] = dq[window, :] + dot(put, grads).astype(jnp.bfloat16)
            for j, ref in enumerate((dk, dv)):
                ref[window, :] = ref[window, :] + dot(put, near_ref[z, j]).astype(jnp.bfloat16)
            return carry

        lax.fori_loop(0, NZ, one, 0, unroll=2)


def attend(turn, n_parts, *refs):
    own_y, owners, masks, wide, near = refs[:5]
    prompts = refs[5 : 5 + n_parts]
    dq, dnear, dprompt, mask_of = refs[5 + n_parts :]
    y = lax.rem(own_y[0] + turn, NY)

    def place(s, carry):
        mask_of[owners[0, s]] = masks[0, s]
        return carry

    lax.fori_loop(0, NY * NZ, place, 0)
    key_at = lax.broadcasted_iota(jnp.int32, (SPAN, GROUP * SPAN), 0)
    token_at = lax.broadcasted_iota(jnp.int32, (SPAN, GROUP * SPAN), 1) % SPAN
    near_bias = jnp.where(key_at <= token_at, 0.0, far_below)

    def response(z, prompt_ref, z_in):
        q, g = wide[z, 0], wide[z, 1]
        k = jnp.concatenate([prompt_ref[z_in, :, 0].reshape(PROMPT, HEAD_DIMENSION), near[z, 0]])
        v = jnp.concatenate([prompt_ref[z_in, :, 1].reshape(PROMPT, HEAD_DIMENSION), near[z, 1]])
        scores = dot(k, q, ((1,), (1,)))
        dots = dot(v, g, ((1,), (1,)))
        far_bias = jnp.where(mask_of[z * NY + y] > 0, 0.0, far_below).astype(jnp.float32)
        scores = jnp.concatenate([scores[:PROMPT] + far_bias, scores[PROMPT:] + near_bias], axis=0)
        highest = jnp.max(scores, axis=0, keepdims=True)
        weights = jnp.exp2((scores - highest) * exp2_scale)
        inverse = 1.0 / jnp.sum(weights, axis=0, keepdims=True)
        delta = jnp.sum(weights * dots, axis=0, keepdims=True) * inverse
        probs = weights * inverse
        slopes = (probs * (dots - delta)).astype(jnp.bfloat16)
        probs = probs.astype(jnp.bfloat16)
        k_grad = (dot(slopes, q) * scale).astype(jnp.bfloat16)
        v_grad = dot(probs, g).astype(jnp.bfloat16)
        dq[z] = (dot(slopes, k, ((0,), (0,))) * scale).astype(jnp.bfloat16)
        dprompt[z, :, :HEAD_DIMENSION] = k_grad[:PROMPT]
        dprompt[z, :, HEAD_DIMENSION:] = v_grad[:PROMPT]
        dnear[z, 0] = k_grad[PROMPT:]
        dnear[z, 1] = v_grad[PROMPT:]

    per_part = NZ // n_parts
    for part, prompt_ref in enumerate(prompts):

        def pair(i, carry):
            for j in range(2):
                response(part * per_part + 2 * i + j, prompt_ref, 2 * i + j)
            return carry

        lax.fori_loop(0, per_part // 2, pair, 0)


smem = pl.BlockSpec(memory_space=pltpu.SMEM)
vmem = pl.BlockSpec(memory_space=pltpu.VMEM)


def shaped(*shape):
    return jax.ShapeDtypeStruct(shape, jnp.bfloat16)


def call(body, outs, n_smem, n_vmem, n_scratch, flops, moved):
    return pl.pallas_call(
        body,
        out_shape=outs,
        in_specs=[smem] * n_smem + [vmem] * n_vmem,
        out_specs=[vmem] * len(outs),
        scratch_shapes=[pltpu.SMEM((NY * NZ,), jnp.int32)] * n_scratch,
        compiler_params=pltpu.CompilerParams(vmem_limit_bytes=24 * 1024 * 1024),
        cost_estimate=pl.CostEstimate(flops=flops, bytes_accessed=moved, transcendentals=0),
    )


def pack_call(turns, *args):
    n = len(turns)
    outs = [shaped(NZ, 2, GROUP * SPAN, HEAD_DIMENSION)] * n
    outs += [shaped(NZ, 2, SPAN, HEAD_DIMENSION)] * n
    got = call(functools.partial(pack, turns), outs, 3, 4, 2, 10**9, 8 * 2**20)(*args)
    return got[:n], got[n:]


def unpack_call(turns, own_y, lengths, owners, wide, near, rows):
    outs = [shaped(rows, GROUP * HEAD_DIMENSION)] + [shaped(rows, HEAD_DIMENSION)] * 2
    body = functools.partial(unpack, turns)
    return call(body, outs, 3, 2 * len(turns), 2, 10**9, 4 * 2**20)(
        own_y, lengths, owners, *wide, *near
    )


def attend_call(turn, own_y, owners, masks, wide, near, prompts):
    outs = [
        shaped(NZ, GROUP * SPAN, HEAD_DIMENSION),
        shaped(NZ, 2, SPAN, HEAD_DIMENSION),
        shaped(NZ, PROMPT, 2 * HEAD_DIMENSION),
    ]
    body = functools.partial(attend, turn, len(prompts))
    return call(body, outs, 3, 2 + len(prompts), 1, 3 * 10**9, 4 * 2**20)(
        own_y, owners, masks, wide, near, *prompts
    )


def along_y(turn):
    return [(z * NY + y, z * NY + (y + turn) % NY) for z in range(NZ) for y in range(NY)]


same_y_head = [[(z * NY + y) * HEADS + h for z in range(NZ) for h in range(HEADS)] for y in range(NY)]
same_y = [[z * NY + y for z in range(NZ)] for y in range(NY)]


def per_device(
    queries,
    response_keys,
    response_values,
    output_cotangent,
    prompt_key_rows,
    prompt_value_rows,
    resp_len,
    resp_owner,
    block_mask,
):
    part = prompt_key_rows.shape[0]
    mine = jnp.stack(
        [
            a.reshape(part, HEADS, HEAD_DIMENSION).transpose(1, 0, 2)
            for a in (prompt_key_rows, prompt_value_rows)
        ],
        axis=1,
    )
    mine = jnp.broadcast_to(mine[None], (NZ,) + mine.shape).reshape((NZ * HEADS,) + mine.shape[1:])
    column = lax.all_to_all(
        mine,
        ("dp", "head"),
        split_axis=0,
        concat_axis=0,
        axis_index_groups=same_y_head,
        tiled=True,
    ).reshape(NZ, HEADS, 2, part, HEAD_DIMENSION)
    turns = (0, 1, 3, 2)
    own_y = lax.rem(lax.axis_index("dp"), NY).reshape(1).astype(jnp.int32)
    masks = block_mask.reshape(block_mask.shape[:2])
    wide, near = pack_call(
        turns, own_y, resp_len, resp_owner, queries, output_cotangent, response_keys, response_values
    )
    after = lax.ppermute(column, "dp", along_y(-1))
    before = lax.ppermute(column, "dp", along_y(1))
    half = NZ // 2
    across = [
        lax.ppermute(after[:half], "dp", along_y(-1)),
        lax.ppermute(before[half:], "dp", along_y(1)),
    ]
    dq, dnear, parts = [], [], []
    for turn, a, b, prompts in zip(turns, wide, near, ([column], [after], [before], across)):
        q_part, near_part, prompt_part = attend_call(turn, own_y, resp_owner, masks, a, b, prompts)
        dq.append(q_part)
        dnear.append(near_part)
        parts.append(lax.ppermute(prompt_part, "dp", along_y(turn)) if turn else prompt_part)
    dq, dk, dv = unpack_call(turns, own_y, resp_len, resp_owner, dq, dnear, queries.shape[0])
    summed = sum(a.astype(jnp.float32) for a in parts).astype(jnp.bfloat16)
    shares = lax.all_to_all(
        summed, "dp", split_axis=0, concat_axis=0, axis_index_groups=same_y, tiled=True
    )
    whole = jnp.sum(shares.astype(jnp.float32), axis=0).astype(jnp.bfloat16)
    return (dq, dk, dv, whole[:, :HEAD_DIMENSION], whole[:, HEAD_DIMENSION:])


def solution(mesh):
    placed = (
        P("dp", "head"),
        P("dp", "head"),
        P("dp", "head"),
        P("dp", "head"),
        P(("dp", "head"), None),
        P(("dp", "head"), None),
        P("dp", None),
        P("dp", None),
        P("dp", None, None),
    )
    return jax.shard_map(
        per_device,
        mesh=mesh,
        in_specs=placed,
        out_specs=(
            P("dp", "head"),
            P("dp", "head"),
            P("dp", "head"),
            P("dp", "head"),
            P("dp", "head"),
        ),
        check_vma=False,
    )
```

```python
import functools
import math

import jax
import jax.numpy as jnp
from jax import lax
from jax.experimental import pallas as pl
from jax.experimental.pallas import tpu as pltpu
from jax.sharding import PartitionSpec as P

QUERY_HEADS = 64
KEY_VALUE_HEADS = 8
HEAD_DIMENSION = 128
GROUP = QUERY_HEADS // KEY_VALUE_HEADS
PROMPT = 128
SPAN = 32
WINDOW = 48
NY = 4
NZ = 8
HEADS = 8

far_below = -1e30
scale = 1.0 / math.sqrt(HEAD_DIMENSION)
exp2_scale = scale * math.log2(math.e)


def one_hot(shape, token_dim, offset, length):
    token = lax.broadcasted_iota(jnp.int32, shape, token_dim)
    place = lax.broadcasted_iota(jnp.int32, shape, 1 - token_dim)
    hit = (place == token + offset) & (token < length)
    return jnp.where(hit, 1.0, 0.0).astype(jnp.bfloat16)


def dot(a, b, dims=((1,), (0,))):
    return lax.dot_general(a, b, (dims, ((), ())), preferred_element_type=jnp.float32)


def locate(lengths, owners, masks, first_of, count_of, mask_of):
    def place(s, start):
        owner = owners[0, s]
        first_of[owner] = start
        count_of[owner] = lengths[0, s]
        if mask_of is not None:
            mask_of[owner] = masks[0, s]
        return start + lengths[0, s]

    lax.fori_loop(0, NY * NZ, place, jnp.int32(0))


def window_of(start, rows):
    base = pl.multiple_of(jnp.minimum((start // 16) * 16, rows - WINDOW), 16)
    return pl.ds(base, WINDOW), start - base


def pack(turns, own_y, lengths, owners, query, cotangent, key, value, *refs):
    n = len(turns)
    wide, near = refs[:n], refs[n : 2 * n]
    first_of, count_of = refs[2 * n :]
    locate(lengths, owners, None, first_of, count_of, None)
    rows = query.shape[0]
    for turn, wide_ref, near_ref in zip(turns, wide, near):
        y = lax.rem(own_y[0] + turn, NY)

        def one(z, carry):
            prompt = z * NY + y
            start = first_of[prompt]
            window, offset = window_of(start, rows)
            pick = one_hot((SPAN, WINDOW), 0, offset, count_of[prompt])
            for j, ref in enumerate((query, cotangent)):
                taken = dot(pick, ref[window, :]).astype(jnp.bfloat16)
                for h in range(GROUP):
                    wide_ref[z, j, h * SPAN : (h + 1) * SPAN, :] = taken[
                        :, h * HEAD_DIMENSION : (h + 1) * HEAD_DIMENSION
                    ]
            for j, ref in enumerate((key, value)):
                near_ref[z, j] = dot(pick, ref[window, :]).astype(jnp.bfloat16)
            return carry

        lax.fori_loop(0, NZ, one, 0, unroll=2)


def unpack(pieces, own_y, lengths, owners, *refs):
    n = len(pieces)
    wide, near = refs[:n], refs[n : 2 * n]
    dq, dk, dv, first_of, count_of = refs[2 * n :]
    locate(lengths, owners, None, first_of, count_of, None)
    rows = dq.shape[0]
    dq[...] = jnp.zeros_like(dq)
    dk[...] = jnp.zeros_like(dk)
    dv[...] = jnp.zeros_like(dv)
    for (turn, first), wide_ref, near_ref in zip(pieces, wide, near):
        y = lax.rem(own_y[0] + turn, NY)

        def one(i, carry):
            prompt = (first + i) * NY + y
            window, offset = window_of(first_of[prompt], rows)
            put = one_hot((WINDOW, SPAN), 1, offset, count_of[prompt])
            grads = jnp.concatenate(
                [wide_ref[i, h * SPAN : (h + 1) * SPAN, :] for h in range(GROUP)], axis=1
            )
            dq[window, :] = dq[window, :] + dot(put, grads).astype(jnp.bfloat16)
            for j, ref in enumerate((dk, dv)):
                ref[window, :] = ref[window, :] + dot(put, near_ref[i, j]).astype(jnp.bfloat16)
            return carry

        lax.fori_loop(0, wide_ref.shape[0], one, 0, unroll=2)


def attend(turn, first, *refs):
    own_y, owners, masks, wide, near, prompts, dq, dnear, dprompt, mask_of = refs
    y = lax.rem(own_y[0] + turn, NY)

    def place(s, carry):
        mask_of[owners[0, s]] = masks[0, s]
        return carry

    lax.fori_loop(0, NY * NZ, place, 0, unroll=4)
    key_at = lax.broadcasted_iota(jnp.int32, (SPAN, GROUP * SPAN), 0)
    token_at = lax.broadcasted_iota(jnp.int32, (SPAN, GROUP * SPAN), 1) % SPAN
    near_bias = jnp.where(key_at <= token_at, 0.0, far_below)
    for i in range(prompts.shape[0]):
        z = first + i
        q, g = wide[z, 0], wide[z, 1]
        k = jnp.concatenate([prompts[i, :, 0].reshape(PROMPT, HEAD_DIMENSION), near[z, 0]])
        v = jnp.concatenate([prompts[i, :, 1].reshape(PROMPT, HEAD_DIMENSION), near[z, 1]])
        scores = dot(k, q, ((1,), (1,)))
        dots = dot(v, g, ((1,), (1,)))
        far_bias = jnp.where(mask_of[z * NY + y] > 0, 0.0, far_below).astype(jnp.float32)
        scores = jnp.concatenate([scores[:PROMPT] + far_bias, scores[PROMPT:] + near_bias], axis=0)
        highest = jnp.max(scores, axis=0, keepdims=True)
        weights = jnp.exp2((scores - highest) * exp2_scale)
        inverse = 1.0 / jnp.sum(weights, axis=0, keepdims=True)
        delta = jnp.sum(weights * dots, axis=0, keepdims=True) * inverse
        probs = weights * inverse
        slopes = (probs * (dots - delta)).astype(jnp.bfloat16)
        probs = probs.astype(jnp.bfloat16)
        k_grad = (dot(slopes, q) * scale).astype(jnp.bfloat16)
        v_grad = dot(probs, g).astype(jnp.bfloat16)
        dq[i] = (dot(slopes, k, ((0,), (0,))) * scale).astype(jnp.bfloat16)
        dprompt[i, :, :HEAD_DIMENSION] = k_grad[:PROMPT]
        dprompt[i, :, HEAD_DIMENSION:] = v_grad[:PROMPT]
        dnear[i, 0] = k_grad[PROMPT:]
        dnear[i, 1] = v_grad[PROMPT:]


def spread(keys, values, out):
    part = keys.shape[0]
    for h in range(HEADS):
        for j, ref in enumerate((keys, values)):
            rows = ref[:, h * HEAD_DIMENSION : (h + 1) * HEAD_DIMENSION]
            for z in range(NZ):
                out[z * HEADS + h, j] = rows


smem = pl.BlockSpec(memory_space=pltpu.SMEM)
vmem = pl.BlockSpec(memory_space=pltpu.VMEM)


def shaped(*shape):
    return jax.ShapeDtypeStruct(shape, jnp.bfloat16)


def call(body, outs, n_smem, n_vmem, n_scratch, flops, moved):
    return pl.pallas_call(
        body,
        out_shape=outs,
        in_specs=[smem] * n_smem + [vmem] * n_vmem,
        out_specs=[vmem] * len(outs),
        scratch_shapes=[pltpu.SMEM((NY * NZ,), jnp.int32)] * n_scratch,
        compiler_params=pltpu.CompilerParams(vmem_limit_bytes=24 * 1024 * 1024),
        cost_estimate=pl.CostEstimate(flops=flops, bytes_accessed=moved, transcendentals=0),
    )


def pack_call(turns, *args):
    n = len(turns)
    outs = [shaped(NZ, 2, GROUP * SPAN, HEAD_DIMENSION)] * n
    outs += [shaped(NZ, 2, SPAN, HEAD_DIMENSION)] * n
    got = call(functools.partial(pack, turns), outs, 3, 4, 2, 10**9, 8 * 2**20)(*args)
    return got[:n], got[n:]


def unpack_call(pieces, own_y, lengths, owners, wide, near, rows):
    outs = [shaped(rows, GROUP * HEAD_DIMENSION)] + [shaped(rows, HEAD_DIMENSION)] * 2
    body = functools.partial(unpack, pieces)
    return call(body, outs, 3, 2 * len(pieces), 2, 10**9, 4 * 2**20)(
        own_y, lengths, owners, *wide, *near
    )


def attend_call(turn, first, own_y, owners, masks, wide, near, prompts):
    n = prompts.shape[0]
    outs = [
        shaped(n, GROUP * SPAN, HEAD_DIMENSION),
        shaped(n, 2, SPAN, HEAD_DIMENSION),
        shaped(n, PROMPT, 2 * HEAD_DIMENSION),
    ]
    body = functools.partial(attend, turn, first)
    return call(body, outs, 3, 3, 1, 4 * 10**8 * n, 2**19 * n)(
        own_y, owners, masks, wide, near, prompts
    )


def spread_call(keys, values):
    out = shaped(NZ * HEADS, 2, keys.shape[0], HEAD_DIMENSION)
    return call(spread, [out], 0, 2, 0, 0, 2**19)(keys, values)[0]


def along_y(turn):
    return [(z * NY + y, z * NY + (y + turn) % NY) for z in range(NZ) for y in range(NY)]


same_y_head = [[(z * NY + y) * HEADS + h for z in range(NZ) for h in range(HEADS)] for y in range(NY)]
same_y = [[z * NY + y for z in range(NZ)] for y in range(NY)]


def per_device(
    queries,
    response_keys,
    response_values,
    output_cotangent,
    prompt_key_rows,
    prompt_value_rows,
    resp_len,
    resp_owner,
    block_mask,
):
    part = prompt_key_rows.shape[0]
    half = NZ // 2
    column = lax.all_to_all(
        spread_call(prompt_key_rows, prompt_value_rows),
        ("dp", "head"),
        split_axis=0,
        concat_axis=0,
        axis_index_groups=same_y_head,
        tiled=True,
    ).reshape(NZ, HEADS, 2, part, HEAD_DIMENSION)
    turns = (0, 1, 3, 2)
    own_y = lax.rem(lax.axis_index("dp"), NY).reshape(1).astype(jnp.int32)
    masks = block_mask.reshape(block_mask.shape[:2])
    wide, near = pack_call(
        turns, own_y, resp_len, resp_owner, queries, output_cotangent, response_keys, response_values
    )
    halves = (column[:half], column[half:])
    after = [lax.ppermute(a, "dp", along_y(-1)) for a in halves]
    before = [lax.ppermute(a, "dp", along_y(1)) for a in halves]
    after, before = lax.optimization_barrier((after, before))
    across = [
        lax.ppermute(after[0], "dp", along_y(-1)),
        lax.ppermute(before[1], "dp", along_y(1)),
    ]
    pieces = (
        [(1, 0, after[0]), (3, 0, before[0]), (1, half, after[1]), (3, half, before[1])]
        + [(2, 0, across[0]), (2, half, across[1])]
        + [(0, 0, column)]
    )
    place = {turn: i for i, turn in enumerate(turns)}
    dq, dnear, sums = [], [], [[], []]
    for turn, first, prompts in pieces:
        i = place[turn]
        q_part, near_part, prompt_part = attend_call(
            turn, first, own_y, resp_owner, masks, wide[i], near[i], prompts
        )
        dq.append(q_part)
        dnear.append(near_part)
        if turn:
            sums[first // half].append(lax.ppermute(prompt_part, "dp", along_y(turn)))
        else:
            sums[0].append(prompt_part[:half])
            sums[1].append(prompt_part[half:])
    dq, dk, dv = unpack_call(
        [piece[:2] for piece in pieces], own_y, resp_len, resp_owner, dq, dnear, queries.shape[0]
    )
    summed = jnp.concatenate([sum(a.astype(jnp.float32) for a in part) for part in sums], axis=0)
    summed, dq, dk, dv = lax.optimization_barrier((summed.astype(jnp.bfloat16), dq, dk, dv))
    shares = lax.all_to_all(
        summed, "dp", split_axis=0, concat_axis=0, axis_index_groups=same_y, tiled=True
    )
    whole = jnp.sum(shares.astype(jnp.float32), axis=0).astype(jnp.bfloat16)
    return (dq, dk, dv, whole[:, :HEAD_DIMENSION], whole[:, HEAD_DIMENSION:])


def solution(mesh):
    placed = (
        P("dp", "head"),
        P("dp", "head"),
        P("dp", "head"),
        P("dp", "head"),
        P(("dp", "head"), None),
        P(("dp", "head"), None),
        P("dp", None),
        P("dp", None),
        P("dp", None, None),
    )
    return jax.shard_map(
        per_device,
        mesh=mesh,
        in_specs=placed,
        out_specs=(
            P("dp", "head"),
            P("dp", "head"),
            P("dp", "head"),
            P("dp", "head"),
            P("dp", "head"),
        ),
        check_vma=False,
    )
```

```python
import functools
import math

import jax
import jax.numpy as jnp
from jax import lax
from jax.experimental import pallas as pl
from jax.experimental.pallas import tpu as pltpu
from jax.sharding import PartitionSpec as P

QUERY_HEADS = 64
KEY_VALUE_HEADS = 8
HEAD_DIMENSION = 128
GROUP = QUERY_HEADS // KEY_VALUE_HEADS
PROMPT = 128
SPAN = 32
WINDOW = 48
NY = 4
NZ = 8
HEADS = 8

far_below = -1e30
scale = 1.0 / math.sqrt(HEAD_DIMENSION)
exp2_scale = scale * math.log2(math.e)


def one_hot(shape, token_dim, offset, length):
    token = lax.broadcasted_iota(jnp.int32, shape, token_dim)
    place = lax.broadcasted_iota(jnp.int32, shape, 1 - token_dim)
    hit = (place == token + offset) & (token < length)
    return jnp.where(hit, 1.0, 0.0).astype(jnp.bfloat16)


def dot(a, b, dims=((1,), (0,))):
    return lax.dot_general(a, b, (dims, ((), ())), preferred_element_type=jnp.float32)


def locate(lengths, owners, masks, first_of, count_of, mask_of):
    def place(s, start):
        owner = owners[0, s]
        first_of[owner] = start
        count_of[owner] = lengths[0, s]
        if mask_of is not None:
            mask_of[owner] = masks[0, s]
        return start + lengths[0, s]

    lax.fori_loop(0, NY * NZ, place, jnp.int32(0))


def window_of(start, rows):
    base = pl.multiple_of(jnp.minimum((start // 16) * 16, rows - WINDOW), 16)
    return pl.ds(base, WINDOW), start - base


def pack(turns, own_y, lengths, owners, masks, query, cotangent, key, value, *refs):
    n = len(turns)
    wide, near, bias = refs[:n], refs[n : 2 * n], refs[2 * n : 3 * n]
    first_of, count_of, mask_of = refs[3 * n :]
    locate(lengths, owners, masks, first_of, count_of, mask_of)
    rows = query.shape[0]
    for turn, wide_ref, near_ref, bias_ref in zip(turns, wide, near, bias):
        y = lax.rem(own_y[0] + turn, NY)

        def one(z, carry):
            prompt = z * NY + y
            start = first_of[prompt]
            window, offset = window_of(start, rows)
            pick = one_hot((SPAN, WINDOW), 0, offset, count_of[prompt])
            for j, ref in enumerate((query, cotangent)):
                taken = dot(pick, ref[window, :]).astype(jnp.bfloat16)
                for h in range(GROUP):
                    wide_ref[z, j, h * SPAN : (h + 1) * SPAN, :] = taken[
                        :, h * HEAD_DIMENSION : (h + 1) * HEAD_DIMENSION
                    ]
            for j, ref in enumerate((key, value)):
                near_ref[z, j] = dot(pick, ref[window, :]).astype(jnp.bfloat16)
            hidden = jnp.where(mask_of[prompt] > 0, 0.0, far_below).astype(jnp.float32)
            bias_ref[z] = jnp.full(bias_ref.shape[1:], hidden, jnp.float32)
            return carry

        lax.fori_loop(0, NZ, one, 0, unroll=2)


def unpack(turns, own_y, lengths, owners, *refs):
    n = len(turns)
    wide, near = refs[:n], refs[n : 2 * n]
    dq, dk, dv, first_of, count_of = refs[2 * n :]
    locate(lengths, owners, None, first_of, count_of, None)
    rows = dq.shape[0]
    dq[...] = jnp.zeros_like(dq)
    dk[...] = jnp.zeros_like(dk)
    dv[...] = jnp.zeros_like(dv)
    for turn, wide_ref, near_ref in zip(turns, wide, near):
        y = lax.rem(own_y[0] + turn, NY)

        def one(i, carry):
            prompt = i * NY + y
            window, offset = window_of(first_of[prompt], rows)
            put = one_hot((WINDOW, SPAN), 1, offset, count_of[prompt])
            grads = jnp.concatenate(
                [wide_ref[i, h * SPAN : (h + 1) * SPAN, :] for h in range(GROUP)], axis=1
            )
            dq[window, :] = dq[window, :] + dot(put, grads).astype(jnp.bfloat16)
            for j, ref in enumerate((dk, dv)):
                ref[window, :] = ref[window, :] + dot(put, near_ref[i, j]).astype(jnp.bfloat16)
            return carry

        lax.fori_loop(0, NZ, one, 0, unroll=2)


def attend(n_parts, wide, near, bias, *refs):
    parts = refs[:n_parts]
    dq, dnear, dprompt = refs[n_parts:]
    key_at = lax.broadcasted_iota(jnp.int32, (SPAN, GROUP * SPAN), 0)
    token_at = lax.broadcasted_iota(jnp.int32, (SPAN, GROUP * SPAN), 1) % SPAN
    near_bias = jnp.where(key_at <= token_at, 0.0, far_below)
    per_part = NZ // n_parts
    for z in range(NZ):
        prompt = parts[z // per_part]
        i = z % per_part
        q, g = wide[z, 0], wide[z, 1]
        k = jnp.concatenate([prompt[i, :, 0].reshape(PROMPT, HEAD_DIMENSION), near[z, 0]])
        v = jnp.concatenate([prompt[i, :, 1].reshape(PROMPT, HEAD_DIMENSION), near[z, 1]])
        scores = dot(k, q, ((1,), (1,)))
        dots = dot(v, g, ((1,), (1,)))
        far, own = scores[:PROMPT], scores[PROMPT:] + near_bias
        hidden = bias[z]
        highest = jnp.maximum(
            jnp.max(far, axis=0, keepdims=True) + hidden, jnp.max(own, axis=0, keepdims=True)
        )
        weights = jnp.exp2(
            jnp.concatenate([far - (highest - hidden), own - highest], axis=0) * exp2_scale
        )
        inverse = 1.0 / jnp.sum(weights, axis=0, keepdims=True)
        delta = jnp.sum(weights * dots, axis=0, keepdims=True) * inverse
        probs = weights * inverse
        slopes = (probs * (dots - delta)).astype(jnp.bfloat16)
        probs = probs.astype(jnp.bfloat16)
        k_grad = (dot(slopes, q) * scale).astype(jnp.bfloat16)
        v_grad = dot(probs, g).astype(jnp.bfloat16)
        dq[z] = (dot(slopes, k, ((0,), (0,))) * scale).astype(jnp.bfloat16)
        dprompt[z, :, :HEAD_DIMENSION] = k_grad[:PROMPT]
        dprompt[z, :, HEAD_DIMENSION:] = v_grad[:PROMPT]
        dnear[z, 0] = k_grad[PROMPT:]
        dnear[z, 1] = v_grad[PROMPT:]


def spread(keys, values, out, held, sems):
    copies = [
        pltpu.make_async_copy(ref, held.at[j], sems.at[j]) for j, ref in enumerate((keys, values))
    ]
    for copy in copies:
        copy.start()
    for j, copy in enumerate(copies):
        copy.wait()
        for h in range(HEADS):
            rows = held[j, :, h * HEAD_DIMENSION : (h + 1) * HEAD_DIMENSION]
            for z in range(NZ):
                out[z * HEADS + h, j] = rows


smem = pl.BlockSpec(memory_space=pltpu.SMEM)
vmem = pl.BlockSpec(memory_space=pltpu.VMEM)


def shaped(*shape):
    return jax.ShapeDtypeStruct(shape, jnp.bfloat16)


def call(body, outs, n_smem, n_vmem, n_scratch, flops, moved):
    return pl.pallas_call(
        body,
        out_shape=outs,
        in_specs=[smem] * n_smem + [vmem] * n_vmem,
        out_specs=[vmem] * len(outs),
        scratch_shapes=[pltpu.SMEM((NY * NZ,), jnp.int32)] * n_scratch,
        compiler_params=pltpu.CompilerParams(vmem_limit_bytes=24 * 1024 * 1024),
        cost_estimate=pl.CostEstimate(flops=flops, bytes_accessed=moved, transcendentals=0),
    )


def pack_call(turns, *args):
    n = len(turns)
    outs = [shaped(NZ, 2, GROUP * SPAN, HEAD_DIMENSION)] * n
    outs += [shaped(NZ, 2, SPAN, HEAD_DIMENSION)] * n
    outs += [jax.ShapeDtypeStruct((NZ, 1, GROUP * SPAN), jnp.float32)] * n
    got = call(functools.partial(pack, turns), outs, 4, 4, 3, 10**9, 8 * 2**20)(*args)
    return [got[i::n] for i in range(n)]


def unpack_call(turns, own_y, lengths, owners, wide, near, rows):
    outs = [shaped(rows, GROUP * HEAD_DIMENSION)] + [shaped(rows, HEAD_DIMENSION)] * 2
    body = functools.partial(unpack, turns)
    return call(body, outs, 3, 2 * len(turns), 2, 10**9, 4 * 2**20)(
        own_y, lengths, owners, *wide, *near
    )


def attend_call(packed, parts):
    outs = [
        shaped(NZ, GROUP * SPAN, HEAD_DIMENSION),
        shaped(NZ, 2, SPAN, HEAD_DIMENSION),
        shaped(NZ, PROMPT, 2 * HEAD_DIMENSION),
    ]
    body = functools.partial(attend, len(parts))
    return call(body, outs, 0, 3 + len(parts), 0, 4 * 10**9, 2**22)(*packed, *parts)


def spread_call(keys, values):
    anywhere = pl.BlockSpec(memory_space=pl.ANY)
    return pl.pallas_call(
        spread,
        out_shape=shaped(NZ * HEADS, 2, keys.shape[0], HEAD_DIMENSION),
        in_specs=[anywhere] * 2,
        out_specs=vmem,
        scratch_shapes=[
            pltpu.VMEM((2,) + keys.shape, jnp.bfloat16),
            pltpu.SemaphoreType.DMA((2,)),
        ],
        compiler_params=pltpu.CompilerParams(vmem_limit_bytes=60 * 1024 * 1024),
    )(keys, values)


def along_y(turn):
    return [(z * NY + y, z * NY + (y + turn) % NY) for z in range(NZ) for y in range(NY)]


same_y_head = [[(z * NY + y) * HEADS + h for z in range(NZ) for h in range(HEADS)] for y in range(NY)]
same_y = [[z * NY + y for z in range(NZ)] for y in range(NY)]


def per_device(
    queries,
    response_keys,
    response_values,
    output_cotangent,
    prompt_key_rows,
    prompt_value_rows,
    resp_len,
    resp_owner,
    block_mask,
):
    part = prompt_key_rows.shape[0]
    half = NZ // 2
    column = lax.all_to_all(
        spread_call(prompt_key_rows, prompt_value_rows),
        ("dp", "head"),
        split_axis=0,
        concat_axis=0,
        axis_index_groups=same_y_head,
        tiled=True,
    ).reshape(NZ, HEADS, 2, part, HEAD_DIMENSION)
    turns = (0, 1, 3, 2)
    own_y = lax.rem(lax.axis_index("dp"), NY).reshape(1).astype(jnp.int32)
    masks = block_mask.reshape(block_mask.shape[:2])
    own, next_one, last_one, far = pack_call(
        turns,
        own_y,
        resp_len,
        resp_owner,
        masks,
        queries,
        output_cotangent,
        response_keys,
        response_values,
    )
    halves = (column[:half], lax.optimization_barrier(column)[half:])
    after = [lax.ppermute(a, "dp", along_y(-1)) for a in halves]
    before = [lax.ppermute(a, "dp", along_y(1)) for a in halves]
    after, before = lax.optimization_barrier((after, before))
    across = [
        lax.ppermute(after[0], "dp", along_y(-1)),
        lax.ppermute(before[1], "dp", along_y(1)),
    ]
    dq, dnear, sums = [], [], []
    for turn, packed, prompts in (
        (1, next_one, after),
        (3, last_one, before),
        (2, far, across),
        (0, own, [column]),
    ):
        q_part, near_part, prompt_part = attend_call(packed, prompts)
        dq.append(q_part)
        dnear.append(near_part)
        sums.append(lax.ppermute(prompt_part, "dp", along_y(turn)) if turn else prompt_part)
    dq, dk, dv = unpack_call(
        (1, 3, 2, 0), own_y, resp_len, resp_owner, dq, dnear, queries.shape[0]
    )
    summed = sum(a.astype(jnp.float32) for a in sums).astype(jnp.bfloat16)
    summed, dq, dk, dv = lax.optimization_barrier((summed, dq, dk, dv))
    shares = lax.all_to_all(
        summed, "dp", split_axis=0, concat_axis=0, axis_index_groups=same_y, tiled=True
    )
    whole = jnp.sum(shares.astype(jnp.float32), axis=0).astype(jnp.bfloat16)
    return (dq, dk, dv, whole[:, :HEAD_DIMENSION], whole[:, HEAD_DIMENSION:])


def solution(mesh):
    placed = (
        P("dp", "head"),
        P("dp", "head"),
        P("dp", "head"),
        P("dp", "head"),
        P(("dp", "head"), None),
        P(("dp", "head"), None),
        P("dp", None),
        P("dp", None),
        P("dp", None, None),
    )
    return jax.shard_map(
        per_device,
        mesh=mesh,
        in_specs=placed,
        out_specs=(
            P("dp", "head"),
            P("dp", "head"),
            P("dp", "head"),
            P("dp", "head"),
            P("dp", "head"),
        ),
        check_vma=False,
    )
```

```python
import functools
import math

import jax
import jax.numpy as jnp
from jax import lax
from jax.experimental import pallas as pl
from jax.experimental.pallas import tpu as pltpu
from jax.sharding import PartitionSpec as P

QUERY_HEADS = 64
KEY_VALUE_HEADS = 8
HEAD_DIMENSION = 128
GROUP = QUERY_HEADS // KEY_VALUE_HEADS
PROMPT = 128
SPAN = 32
WINDOW = 48
NY = 4
NZ = 8
HEADS = 8

far_below = -1e30
scale = 1.0 / math.sqrt(HEAD_DIMENSION)
exp2_scale = scale * math.log2(math.e)


def one_hot(shape, token_dim, offset, length):
    token = lax.broadcasted_iota(jnp.int32, shape, token_dim)
    place = lax.broadcasted_iota(jnp.int32, shape, 1 - token_dim)
    hit = (place == token + offset) & (token < length)
    return jnp.where(hit, 1.0, 0.0).astype(jnp.bfloat16)


def dot(a, b, dims=((1,), (0,))):
    return lax.dot_general(a, b, (dims, ((), ())), preferred_element_type=jnp.float32)


def locate(lengths, owners, masks, first_of, count_of, mask_of):
    def place(s, start):
        owner = owners[0, s]
        first_of[owner] = start
        count_of[owner] = lengths[0, s]
        if mask_of is not None:
            mask_of[owner] = masks[0, s]
        return start + lengths[0, s]

    lax.fori_loop(0, NY * NZ, place, jnp.int32(0))


def window_of(start, rows):
    base = pl.multiple_of(jnp.minimum((start // 16) * 16, rows - WINDOW), 16)
    return pl.ds(base, WINDOW), start - base


def pack(turns, own_y, lengths, owners, masks, query, cotangent, key, value, *refs):
    n = len(turns)
    wide, near, bias = refs[:n], refs[n : 2 * n], refs[2 * n : 3 * n]
    first_of, count_of, mask_of = refs[3 * n :]
    locate(lengths, owners, masks, first_of, count_of, mask_of)
    rows = query.shape[0]
    for turn, wide_ref, near_ref, bias_ref in zip(turns, wide, near, bias):
        y = lax.rem(own_y[0] + turn, NY)

        def one(z, carry):
            prompt = z * NY + y
            start = first_of[prompt]
            window, offset = window_of(start, rows)
            pick = one_hot((SPAN, WINDOW), 0, offset, count_of[prompt])
            for j, ref in enumerate((query, cotangent)):
                taken = dot(pick, ref[window, :]).astype(jnp.bfloat16)
                for h in range(GROUP):
                    wide_ref[z, j, h * SPAN : (h + 1) * SPAN, :] = taken[
                        :, h * HEAD_DIMENSION : (h + 1) * HEAD_DIMENSION
                    ]
            for j, ref in enumerate((key, value)):
                near_ref[z, j] = dot(pick, ref[window, :]).astype(jnp.bfloat16)
            hidden = jnp.where(mask_of[prompt] > 0, 0.0, far_below).astype(jnp.float32)
            bias_ref[z] = jnp.full(bias_ref.shape[1:], hidden, jnp.float32)
            return carry

        lax.fori_loop(0, NZ, one, 0, unroll=2)


def unpack(turns, own_y, lengths, owners, *refs):
    n = len(turns)
    wide, near = refs[:n], refs[n : 2 * n]
    dq, dk, dv, first_of, count_of = refs[2 * n :]
    locate(lengths, owners, None, first_of, count_of, None)
    rows = dq.shape[0]
    dq[...] = jnp.zeros_like(dq)
    dk[...] = jnp.zeros_like(dk)
    dv[...] = jnp.zeros_like(dv)
    for turn, wide_ref, near_ref in zip(turns, wide, near):
        y = lax.rem(own_y[0] + turn, NY)

        def one(i, carry):
            prompt = i * NY + y
            window, offset = window_of(first_of[prompt], rows)
            put = one_hot((WINDOW, SPAN), 1, offset, count_of[prompt])
            grads = jnp.concatenate(
                [wide_ref[i, h * SPAN : (h + 1) * SPAN, :] for h in range(GROUP)], axis=1
            )
            dq[window, :] = dq[window, :] + dot(put, grads).astype(jnp.bfloat16)
            for j, ref in enumerate((dk, dv)):
                ref[window, :] = ref[window, :] + dot(put, near_ref[i, j]).astype(jnp.bfloat16)
            return carry

        lax.fori_loop(0, NZ, one, 0, unroll=2)


def attend(n_parts, wide, near, bias, *refs):
    parts = refs[:n_parts]
    dq, dnear, dprompt = refs[n_parts:]
    key_at = lax.broadcasted_iota(jnp.int32, (SPAN, GROUP * SPAN), 0)
    token_at = lax.broadcasted_iota(jnp.int32, (SPAN, GROUP * SPAN), 1) % SPAN
    near_bias = jnp.where(key_at <= token_at, 0.0, far_below)
    per_part = NZ // n_parts
    for z in range(NZ):
        prompt = parts[z // per_part]
        i = z % per_part
        q, g = wide[z, 0], wide[z, 1]
        k = jnp.concatenate([prompt[i, :, 0].reshape(PROMPT, HEAD_DIMENSION), near[z, 0]])
        v = jnp.concatenate([prompt[i, :, 1].reshape(PROMPT, HEAD_DIMENSION), near[z, 1]])
        scores = dot(k, q, ((1,), (1,)))
        dots = dot(v, g, ((1,), (1,)))
        far, own = scores[:PROMPT], scores[PROMPT:] + near_bias
        hidden = bias[z]
        highest = jnp.maximum(
            jnp.max(far, axis=0, keepdims=True) + hidden, jnp.max(own, axis=0, keepdims=True)
        )
        weights = jnp.exp2(
            jnp.concatenate([far - (highest - hidden), own - highest], axis=0) * exp2_scale
        )
        inverse = 1.0 / jnp.sum(weights, axis=0, keepdims=True)
        delta = jnp.sum(weights * dots, axis=0, keepdims=True) * inverse
        probs = weights * inverse
        slopes = (probs * (dots - delta)).astype(jnp.bfloat16)
        probs = probs.astype(jnp.bfloat16)
        k_grad = (dot(slopes, q) * scale).astype(jnp.bfloat16)
        v_grad = dot(probs, g).astype(jnp.bfloat16)
        dq[z] = (dot(slopes, k, ((0,), (0,))) * scale).astype(jnp.bfloat16)
        dprompt[z, :, :HEAD_DIMENSION] = k_grad[:PROMPT]
        dprompt[z, :, HEAD_DIMENSION:] = v_grad[:PROMPT]
        dnear[z, 0] = k_grad[PROMPT:]
        dnear[z, 1] = v_grad[PROMPT:]


def spread(keys, values, out, held, sems):
    copies = [
        pltpu.make_async_copy(ref, held.at[j], sems.at[j]) for j, ref in enumerate((keys, values))
    ]
    for copy in copies:
        copy.start()
    for j, copy in enumerate(copies):
        copy.wait()
        for h in range(HEADS):
            rows = held[j, :, h * HEAD_DIMENSION : (h + 1) * HEAD_DIMENSION]
            for z in range(NZ):
                out[z * HEADS + h, j] = rows


smem = pl.BlockSpec(memory_space=pltpu.SMEM)
vmem = pl.BlockSpec(memory_space=pltpu.VMEM)


def shaped(*shape):
    return jax.ShapeDtypeStruct(shape, jnp.bfloat16)


def call(body, outs, n_smem, n_vmem, n_scratch, flops, moved):
    return pl.pallas_call(
        body,
        out_shape=outs,
        in_specs=[smem] * n_smem + [vmem] * n_vmem,
        out_specs=[vmem] * len(outs),
        scratch_shapes=[pltpu.SMEM((NY * NZ,), jnp.int32)] * n_scratch,
        compiler_params=pltpu.CompilerParams(vmem_limit_bytes=24 * 1024 * 1024),
        cost_estimate=pl.CostEstimate(flops=flops, bytes_accessed=moved, transcendentals=0),
    )


def pack_call(turns, *args):
    n = len(turns)
    outs = [shaped(NZ, 2, GROUP * SPAN, HEAD_DIMENSION)] * n
    outs += [shaped(NZ, 2, SPAN, HEAD_DIMENSION)] * n
    outs += [jax.ShapeDtypeStruct((NZ, 1, GROUP * SPAN), jnp.float32)] * n
    got = call(functools.partial(pack, turns), outs, 4, 4, 3, 10**8, 2**10)(*args)
    return [got[i::n] for i in range(n)]


def unpack_call(turns, own_y, lengths, owners, wide, near, rows):
    outs = [shaped(rows, GROUP * HEAD_DIMENSION)] + [shaped(rows, HEAD_DIMENSION)] * 2
    body = functools.partial(unpack, turns)
    return call(body, outs, 3, 2 * len(turns), 2, 10**6, 2**10)(
        own_y, lengths, owners, *wide, *near
    )


def attend_call(packed, parts):
    outs = [
        shaped(NZ, GROUP * SPAN, HEAD_DIMENSION),
        shaped(NZ, 2, SPAN, HEAD_DIMENSION),
        shaped(NZ, PROMPT, 2 * HEAD_DIMENSION),
    ]
    body = functools.partial(attend, len(parts))
    return call(body, outs, 0, 3 + len(parts), 0, 10**6, 2**10)(*packed, *parts)


def split_call(column):
    half = NZ // 2

    def split(column, low, high):
        low[...] = column[:half]
        high[...] = column[half:]

    outs = [shaped(half, *column.shape[1:])] * 2
    return call(split, outs, 0, 1, 0, 0, 2**20)(column)


def spread_call(keys, values):
    anywhere = pl.BlockSpec(memory_space=pl.ANY)
    return pl.pallas_call(
        spread,
        out_shape=shaped(NZ * HEADS, 2, keys.shape[0], HEAD_DIMENSION),
        in_specs=[anywhere] * 2,
        out_specs=vmem,
        scratch_shapes=[
            pltpu.VMEM((2,) + keys.shape, jnp.bfloat16),
            pltpu.SemaphoreType.DMA((2,)),
        ],
        compiler_params=pltpu.CompilerParams(vmem_limit_bytes=60 * 1024 * 1024),
    )(keys, values)


def along_y(turn):
    return [(z * NY + y, z * NY + (y + turn) % NY) for z in range(NZ) for y in range(NY)]


same_y_head = [[(z * NY + y) * HEADS + h for z in range(NZ) for h in range(HEADS)] for y in range(NY)]
same_y = [[z * NY + y for z in range(NZ)] for y in range(NY)]


def per_device(
    queries,
    response_keys,
    response_values,
    output_cotangent,
    prompt_key_rows,
    prompt_value_rows,
    resp_len,
    resp_owner,
    block_mask,
):
    part = prompt_key_rows.shape[0]
    half = NZ // 2
    column = lax.all_to_all(
        spread_call(prompt_key_rows, prompt_value_rows),
        ("dp", "head"),
        split_axis=0,
        concat_axis=0,
        axis_index_groups=same_y_head,
        tiled=True,
    ).reshape(NZ, HEADS, 2, part, HEAD_DIMENSION)
    turns = (0, 1, 3, 2)
    own_y = lax.rem(lax.axis_index("dp"), NY).reshape(1).astype(jnp.int32)
    masks = block_mask.reshape(block_mask.shape[:2])
    own, next_one, last_one, far = pack_call(
        turns,
        own_y,
        resp_len,
        resp_owner,
        masks,
        queries,
        output_cotangent,
        response_keys,
        response_values,
    )
    column, own = lax.optimization_barrier((column, own))
    low, high = split_call(column)
    after_low = lax.ppermute(low, "dp", along_y(-1))
    before_high = lax.ppermute(high, "dp", along_y(1))
    across = [
        lax.ppermute(after_low, "dp", along_y(-1)),
        lax.ppermute(before_high, "dp", along_y(1)),
    ]
    after = [after_low, lax.ppermute(high, "dp", along_y(-1))]
    before = [lax.ppermute(low, "dp", along_y(1)), before_high]
    after, before = lax.optimization_barrier((after, before))
    dq, dnear, sums = [], [], []
    order = (1, 2, 3, 0)
    for turn, packed, prompts in (
        (1, next_one, after),
        (2, far, across),
        (3, last_one, before),
        (0, own, [column]),
    ):
        q_part, near_part, prompt_part = attend_call(packed, prompts)
        dq.append(q_part)
        dnear.append(near_part)
        sums.append(lax.ppermute(prompt_part, "dp", along_y(turn)) if turn else prompt_part)
    dq, dk, dv = unpack_call(
        order, own_y, resp_len, resp_owner, dq, dnear, queries.shape[0]
    )
    summed = sum(a.astype(jnp.float32) for a in sums).astype(jnp.bfloat16)
    summed, dq, dk, dv = lax.optimization_barrier((summed, dq, dk, dv))
    shares = lax.all_to_all(
        summed, "dp", split_axis=0, concat_axis=0, axis_index_groups=same_y, tiled=True
    )
    whole = jnp.sum(shares.astype(jnp.float32), axis=0).astype(jnp.bfloat16)
    return (dq, dk, dv, whole[:, :HEAD_DIMENSION], whole[:, HEAD_DIMENSION:])


def solution(mesh):
    placed = (
        P("dp", "head"),
        P("dp", "head"),
        P("dp", "head"),
        P("dp", "head"),
        P(("dp", "head"), None),
        P(("dp", "head"), None),
        P("dp", None),
        P("dp", None),
        P("dp", None, None),
    )
    return jax.shard_map(
        per_device,
        mesh=mesh,
        in_specs=placed,
        out_specs=(
            P("dp", "head"),
            P("dp", "head"),
            P("dp", "head"),
            P("dp", "head"),
            P("dp", "head"),
        ),
        check_vma=False,
    )
```

```python
import functools
import math

import jax
import jax.numpy as jnp
from jax import lax
from jax.experimental import pallas as pl
from jax.experimental.pallas import tpu as pltpu
from jax.sharding import PartitionSpec as P

QUERY_HEADS = 64
KEY_VALUE_HEADS = 8
HEAD_DIMENSION = 128
GROUP = QUERY_HEADS // KEY_VALUE_HEADS
PROMPT = 128
SPAN = 32
WINDOW = 48
NY = 4
NZ = 8
HEADS = 8

far_below = -1e30
scale = 1.0 / math.sqrt(HEAD_DIMENSION)
exp2_scale = scale * math.log2(math.e)


def one_hot(shape, token_dim, offset, length):
    token = lax.broadcasted_iota(jnp.int32, shape, token_dim)
    place = lax.broadcasted_iota(jnp.int32, shape, 1 - token_dim)
    hit = (place == token + offset) & (token < length)
    return jnp.where(hit, 1.0, 0.0).astype(jnp.bfloat16)


def dot(a, b, dims=((1,), (0,))):
    return lax.dot_general(a, b, (dims, ((), ())), preferred_element_type=jnp.float32)


def locate(lengths, owners, masks, first_of, count_of, mask_of):
    def place(s, start):
        owner = owners[0, s]
        first_of[owner] = start
        count_of[owner] = lengths[0, s]
        if mask_of is not None:
            mask_of[owner] = masks[0, s]
        return start + lengths[0, s]

    lax.fori_loop(0, NY * NZ, place, jnp.int32(0))


def window_of(start, rows):
    base = pl.multiple_of(jnp.minimum((start // 16) * 16, rows - WINDOW), 16)
    return pl.ds(base, WINDOW), start - base


def pack(turns, own_y, lengths, owners, masks, query, cotangent, key, value, *refs):
    n = len(turns)
    wide, near, bias = refs[:n], refs[n : 2 * n], refs[2 * n : 3 * n]
    first_of, count_of, mask_of = refs[3 * n :]
    locate(lengths, owners, masks, first_of, count_of, mask_of)
    rows = query.shape[0]
    for turn, wide_ref, near_ref, bias_ref in zip(turns, wide, near, bias):
        y = lax.rem(own_y[0] + turn, NY)

        def one(z, carry):
            prompt = z * NY + y
            start = first_of[prompt]
            window, offset = window_of(start, rows)
            pick = one_hot((SPAN, WINDOW), 0, offset, count_of[prompt])
            for j, ref in enumerate((query, cotangent)):
                taken = dot(pick, ref[window, :]).astype(jnp.bfloat16)
                for h in range(GROUP):
                    wide_ref[z, j, h * SPAN : (h + 1) * SPAN, :] = taken[
                        :, h * HEAD_DIMENSION : (h + 1) * HEAD_DIMENSION
                    ]
            for j, ref in enumerate((key, value)):
                near_ref[z, j] = dot(pick, ref[window, :]).astype(jnp.bfloat16)
            hidden = jnp.where(mask_of[prompt] > 0, 0.0, far_below).astype(jnp.float32)
            bias_ref[z] = jnp.full(bias_ref.shape[1:], hidden, jnp.float32)
            return carry

        lax.fori_loop(0, NZ, one, 0, unroll=2)


def unpack(turns, own_y, lengths, owners, *refs):
    n = len(turns)
    wide, near = refs[:n], refs[n : 2 * n]
    dq, dk, dv, first_of, count_of = refs[2 * n :]
    locate(lengths, owners, None, first_of, count_of, None)
    rows = dq.shape[0]
    dq[...] = jnp.zeros_like(dq)
    dk[...] = jnp.zeros_like(dk)
    dv[...] = jnp.zeros_like(dv)
    for turn, wide_ref, near_ref in zip(turns, wide, near):
        y = lax.rem(own_y[0] + turn, NY)

        def one(i, carry):
            prompt = i * NY + y
            window, offset = window_of(first_of[prompt], rows)
            put = one_hot((WINDOW, SPAN), 1, offset, count_of[prompt])
            turned = wide_ref[i].T
            grads = jnp.concatenate(
                [turned[h * SPAN : (h + 1) * SPAN] for h in range(GROUP)], axis=1
            )
            dq[window, :] = dq[window, :] + dot(put, grads).astype(jnp.bfloat16)
            for j, ref in enumerate((dk, dv)):
                ref[window, :] = ref[window, :] + dot(put, near_ref[i, j]).astype(jnp.bfloat16)
            return carry

        lax.fori_loop(0, NZ, one, 0, unroll=2)


def attend(n_parts, wide, near, bias, *refs):
    parts = refs[:n_parts]
    dq, dnear, dprompt = refs[n_parts:]
    key_at = lax.broadcasted_iota(jnp.int32, (SPAN, GROUP * SPAN), 0)
    token_at = lax.broadcasted_iota(jnp.int32, (SPAN, GROUP * SPAN), 1) % SPAN
    near_bias = jnp.where(key_at <= token_at, 0.0, far_below)
    per_part = NZ // n_parts
    for z in range(NZ):
        prompt = parts[z // per_part]
        i = z % per_part
        q, g = wide[z, 0], wide[z, 1]
        k = jnp.concatenate([prompt[i, :, 0].reshape(PROMPT, HEAD_DIMENSION), near[z, 0]])
        v = jnp.concatenate([prompt[i, :, 1].reshape(PROMPT, HEAD_DIMENSION), near[z, 1]])
        scores = dot(k, q, ((1,), (1,)))
        dots = dot(v, g, ((1,), (1,)))
        far, own = scores[:PROMPT], scores[PROMPT:] + near_bias
        hidden = bias[z]
        highest = jnp.maximum(
            jnp.max(far, axis=0, keepdims=True) + hidden, jnp.max(own, axis=0, keepdims=True)
        )
        weights = jnp.exp2(
            jnp.concatenate([far - (highest - hidden), own - highest], axis=0) * exp2_scale
        )
        inverse = 1.0 / jnp.sum(weights, axis=0, keepdims=True)
        delta = jnp.sum(weights * dots, axis=0, keepdims=True) * inverse
        probs = weights * inverse
        slopes = (probs * (dots - delta)).astype(jnp.bfloat16)
        probs = probs.astype(jnp.bfloat16)
        k_grad = (dot(slopes, q) * scale).astype(jnp.bfloat16)
        v_grad = dot(probs, g).astype(jnp.bfloat16)
        dq[z] = (dot(k, slopes, ((0,), (0,))) * scale).astype(jnp.bfloat16)
        dprompt[z, :, :HEAD_DIMENSION] = k_grad[:PROMPT]
        dprompt[z, :, HEAD_DIMENSION:] = v_grad[:PROMPT]
        dnear[z, 0] = k_grad[PROMPT:]
        dnear[z, 1] = v_grad[PROMPT:]


def spread(keys, values, out, held, sems):
    copies = [
        pltpu.make_async_copy(ref, held.at[j], sems.at[j]) for j, ref in enumerate((keys, values))
    ]
    for copy in copies:
        copy.start()
    for j, copy in enumerate(copies):
        copy.wait()
        for h in range(HEADS):
            rows = held[j, :, h * HEAD_DIMENSION : (h + 1) * HEAD_DIMENSION]
            for z in range(NZ):
                out[z * HEADS + h, j] = rows


smem = pl.BlockSpec(memory_space=pltpu.SMEM)
vmem = pl.BlockSpec(memory_space=pltpu.VMEM)


def shaped(*shape):
    return jax.ShapeDtypeStruct(shape, jnp.bfloat16)


def call(body, outs, n_smem, n_vmem, n_scratch, flops, moved):
    return pl.pallas_call(
        body,
        out_shape=outs,
        in_specs=[smem] * n_smem + [vmem] * n_vmem,
        out_specs=[vmem] * len(outs),
        scratch_shapes=[pltpu.SMEM((NY * NZ,), jnp.int32)] * n_scratch,
        compiler_params=pltpu.CompilerParams(vmem_limit_bytes=24 * 1024 * 1024),
        cost_estimate=pl.CostEstimate(flops=flops, bytes_accessed=moved, transcendentals=0),
    )


def pack_call(turns, *args):
    n = len(turns)
    outs = [shaped(NZ, 2, GROUP * SPAN, HEAD_DIMENSION)] * n
    outs += [shaped(NZ, 2, SPAN, HEAD_DIMENSION)] * n
    outs += [jax.ShapeDtypeStruct((NZ, 1, GROUP * SPAN), jnp.float32)] * n
    got = call(functools.partial(pack, turns), outs, 4, 4, 3, 10**8, 2**10)(*args)
    return [got[i::n] for i in range(n)]


def unpack_call(turns, own_y, lengths, owners, wide, near, rows):
    outs = [shaped(rows, GROUP * HEAD_DIMENSION)] + [shaped(rows, HEAD_DIMENSION)] * 2
    body = functools.partial(unpack, turns)
    return call(body, outs, 3, 2 * len(turns), 2, 10**6, 2**10)(
        own_y, lengths, owners, *wide, *near
    )


def attend_call(packed, parts):
    outs = [
        shaped(NZ, HEAD_DIMENSION, GROUP * SPAN),
        shaped(NZ, 2, SPAN, HEAD_DIMENSION),
        shaped(NZ, PROMPT, 2 * HEAD_DIMENSION),
    ]
    body = functools.partial(attend, len(parts))
    return call(body, outs, 0, 3 + len(parts), 0, 10**6, 2**10)(*packed, *parts)


def split_call(column):
    half = NZ // 2

    def split(column, low, high):
        low[...] = column[:half]
        high[...] = column[half:]

    outs = [shaped(half, *column.shape[1:])] * 2
    return call(split, outs, 0, 1, 0, 0, 2**20)(column)


def spread_call(keys, values):
    anywhere = pl.BlockSpec(memory_space=pl.ANY)
    return pl.pallas_call(
        spread,
        out_shape=shaped(NZ * HEADS, 2, keys.shape[0], HEAD_DIMENSION),
        in_specs=[anywhere] * 2,
        out_specs=vmem,
        scratch_shapes=[
            pltpu.VMEM((2,) + keys.shape, jnp.bfloat16),
            pltpu.SemaphoreType.DMA((2,)),
        ],
        compiler_params=pltpu.CompilerParams(vmem_limit_bytes=60 * 1024 * 1024),
    )(keys, values)


def along_y(turn):
    return [(z * NY + y, z * NY + (y + turn) % NY) for z in range(NZ) for y in range(NY)]


same_y_head = [[(z * NY + y) * HEADS + h for z in range(NZ) for h in range(HEADS)] for y in range(NY)]
same_y = [[z * NY + y for z in range(NZ)] for y in range(NY)]


def per_device(
    queries,
    response_keys,
    response_values,
    output_cotangent,
    prompt_key_rows,
    prompt_value_rows,
    resp_len,
    resp_owner,
    block_mask,
):
    part = prompt_key_rows.shape[0]
    half = NZ // 2
    column = lax.all_to_all(
        spread_call(prompt_key_rows, prompt_value_rows),
        ("dp", "head"),
        split_axis=0,
        concat_axis=0,
        axis_index_groups=same_y_head,
        tiled=True,
    ).reshape(NZ, HEADS, 2, part, HEAD_DIMENSION)
    own_y = lax.rem(lax.axis_index("dp"), NY).reshape(1).astype(jnp.int32)
    masks = block_mask.reshape(block_mask.shape[:2])
    scalars = (own_y, resp_len, resp_owner, masks)
    rows_of = (queries, output_cotangent, response_keys, response_values)
    next_one, last_one = pack_call((1, 3), *scalars, *rows_of)
    far, own = pack_call((2, 0), *scalars, *rows_of)
    column, next_one = lax.optimization_barrier((column, next_one))
    low, high = split_call(column)
    after_low = lax.ppermute(low, "dp", along_y(-1))
    before_high = lax.ppermute(high, "dp", along_y(1))
    across = [
        lax.ppermute(after_low, "dp", along_y(-1)),
        lax.ppermute(before_high, "dp", along_y(1)),
    ]
    after = [after_low, lax.ppermute(high, "dp", along_y(-1))]
    before = [lax.ppermute(low, "dp", along_y(1)), before_high]
    after, before = lax.optimization_barrier((after, before))
    dq, dnear, sums = [], [], []
    order = (1, 2, 3, 0)
    for turn, packed, prompts in (
        (1, next_one, after),
        (2, far, across),
        (3, last_one, before),
        (0, own, [column]),
    ):
        q_part, near_part, prompt_part = attend_call(packed, prompts)
        dq.append(q_part)
        dnear.append(near_part)
        sums.append(lax.ppermute(prompt_part, "dp", along_y(turn)) if turn else prompt_part)
    dq, dk, dv = unpack_call(
        order, own_y, resp_len, resp_owner, dq, dnear, queries.shape[0]
    )
    summed = sum(a.astype(jnp.float32) for a in sums).astype(jnp.bfloat16)
    summed, dq, dk, dv = lax.optimization_barrier((summed, dq, dk, dv))
    shares = lax.all_to_all(
        summed, "dp", split_axis=0, concat_axis=0, axis_index_groups=same_y, tiled=True
    )
    whole = jnp.sum(shares.astype(jnp.float32), axis=0).astype(jnp.bfloat16)
    return (dq, dk, dv, whole[:, :HEAD_DIMENSION], whole[:, HEAD_DIMENSION:])


def solution(mesh):
    placed = (
        P("dp", "head"),
        P("dp", "head"),
        P("dp", "head"),
        P("dp", "head"),
        P(("dp", "head"), None),
        P(("dp", "head"), None),
        P("dp", None),
        P("dp", None),
        P("dp", None, None),
    )
    return jax.shard_map(
        per_device,
        mesh=mesh,
        in_specs=placed,
        out_specs=(
            P("dp", "head"),
            P("dp", "head"),
            P("dp", "head"),
            P("dp", "head"),
            P("dp", "head"),
        ),
        check_vma=False,
    )
```

```python
import functools
import math

import jax
import jax.numpy as jnp
from jax import lax
from jax.experimental import pallas as pl
from jax.experimental.pallas import tpu as pltpu
from jax.sharding import PartitionSpec as P

QUERY_HEADS = 64
KEY_VALUE_HEADS = 8
HEAD_DIMENSION = 128
GROUP = QUERY_HEADS // KEY_VALUE_HEADS
PROMPT = 128
SPAN = 32
WINDOW = 48
NY = 4
NZ = 8
HEADS = 8

far_below = -1e30
scale = 1.0 / math.sqrt(HEAD_DIMENSION)
exp2_scale = scale * math.log2(math.e)


def one_hot(shape, token_dim, offset, length):
    token = lax.broadcasted_iota(jnp.int32, shape, token_dim)
    place = lax.broadcasted_iota(jnp.int32, shape, 1 - token_dim)
    hit = (place == token + offset) & (token < length)
    return jnp.where(hit, 1.0, 0.0).astype(jnp.bfloat16)


def dot(a, b, dims=((1,), (0,))):
    return lax.dot_general(a, b, (dims, ((), ())), preferred_element_type=jnp.float32)


def locate(lengths, owners, masks, first_of, count_of, mask_of):
    def place(s, start):
        owner = owners[0, s]
        first_of[owner] = start
        count_of[owner] = lengths[0, s]
        if mask_of is not None:
            mask_of[owner] = masks[0, s]
        return start + lengths[0, s]

    lax.fori_loop(0, NY * NZ, place, jnp.int32(0))


def window_of(start, rows):
    base = pl.multiple_of(jnp.minimum((start // 16) * 16, rows - WINDOW), 16)
    return pl.ds(base, WINDOW), start - base


def pack(turns, own_y, lengths, owners, masks, query, cotangent, key, value, *refs):
    n = len(turns)
    wide, near, bias = refs[:n], refs[n : 2 * n], refs[2 * n : 3 * n]
    first_of, count_of, mask_of = refs[3 * n :]
    locate(lengths, owners, masks, first_of, count_of, mask_of)
    rows = query.shape[0]
    for turn, wide_ref, near_ref, bias_ref in zip(turns, wide, near, bias):

        def one(z, carry):
            y = lax.rem(own_y[0] + jnp.where(z < NZ // 2, turn[0], turn[1]), NY)
            prompt = z * NY + y
            start = first_of[prompt]
            window, offset = window_of(start, rows)
            pick = one_hot((SPAN, WINDOW), 0, offset, count_of[prompt])
            for j, ref in enumerate((query, cotangent)):
                taken = dot(pick, ref[window, :]).astype(jnp.bfloat16)
                for h in range(GROUP):
                    wide_ref[z, j, h * SPAN : (h + 1) * SPAN, :] = taken[
                        :, h * HEAD_DIMENSION : (h + 1) * HEAD_DIMENSION
                    ]
            for j, ref in enumerate((key, value)):
                near_ref[z, j] = dot(pick, ref[window, :]).astype(jnp.bfloat16)
            hidden = jnp.where(mask_of[prompt] > 0, 0.0, far_below).astype(jnp.float32)
            bias_ref[z] = jnp.full(bias_ref.shape[1:], hidden, jnp.float32)
            return carry

        lax.fori_loop(0, NZ, one, 0, unroll=2)


def unpack(turns, own_y, lengths, owners, *refs):
    n = len(turns)
    wide, near = refs[:n], refs[n : 2 * n]
    dq, dk, dv, first_of, count_of = refs[2 * n :]
    locate(lengths, owners, None, first_of, count_of, None)
    rows = dq.shape[0]
    dq[...] = jnp.zeros_like(dq)
    dk[...] = jnp.zeros_like(dk)
    dv[...] = jnp.zeros_like(dv)
    for turn, wide_ref, near_ref in zip(turns, wide, near):

        def one(i, carry):
            y = lax.rem(own_y[0] + jnp.where(i < NZ // 2, turn[0], turn[1]), NY)
            prompt = i * NY + y
            window, offset = window_of(first_of[prompt], rows)
            put = one_hot((WINDOW, SPAN), 1, offset, count_of[prompt])
            turned = wide_ref[i].T
            grads = jnp.concatenate(
                [turned[h * SPAN : (h + 1) * SPAN] for h in range(GROUP)], axis=1
            )
            dq[window, :] = dq[window, :] + dot(put, grads).astype(jnp.bfloat16)
            for j, ref in enumerate((dk, dv)):
                ref[window, :] = ref[window, :] + dot(put, near_ref[i, j]).astype(jnp.bfloat16)
            return carry

        lax.fori_loop(0, NZ, one, 0, unroll=2)


def attend(n_parts, n_early, n_out, wide, near, bias, *refs):
    parts, early = refs[:n_parts], refs[n_parts : n_parts + n_early]
    dq, dnear, *dprompts = refs[n_parts + n_early :]
    half = NZ // 2
    if n_early:
        dprompts[0][:half] = early[0][...]
        dprompts[1][half:] = early[1][...]
    key_at = lax.broadcasted_iota(jnp.int32, (SPAN, GROUP * SPAN), 0)
    token_at = lax.broadcasted_iota(jnp.int32, (SPAN, GROUP * SPAN), 1) % SPAN
    near_bias = jnp.where(key_at <= token_at, 0.0, far_below)
    per_part = NZ // n_parts
    for z in range(NZ):
        prompt = parts[z // per_part]
        i = z % per_part
        q, g = wide[z, 0], wide[z, 1]
        k = jnp.concatenate([prompt[i, :, 0].reshape(PROMPT, HEAD_DIMENSION), near[z, 0]])
        v = jnp.concatenate([prompt[i, :, 1].reshape(PROMPT, HEAD_DIMENSION), near[z, 1]])
        scores = dot(k, q, ((1,), (1,)))
        dots = dot(v, g, ((1,), (1,)))
        far, own = scores[:PROMPT], scores[PROMPT:] + near_bias
        hidden = bias[z]
        highest = jnp.maximum(
            jnp.max(far, axis=0, keepdims=True) + hidden, jnp.max(own, axis=0, keepdims=True)
        )
        weights = jnp.exp2(
            jnp.concatenate([far - (highest - hidden), own - highest], axis=0) * exp2_scale
        )
        inverse = 1.0 / jnp.sum(weights, axis=0, keepdims=True)
        delta = jnp.sum(weights * dots, axis=0, keepdims=True) * inverse
        probs = weights * inverse
        slopes = (probs * (dots - delta)).astype(jnp.bfloat16)
        probs = probs.astype(jnp.bfloat16)
        k_grad = (dot(slopes, q) * scale).astype(jnp.bfloat16)
        v_grad = dot(probs, g).astype(jnp.bfloat16)
        dq[z] = (dot(k, slopes, ((0,), (0,))) * scale).astype(jnp.bfloat16)
        if n_early:
            dprompt, j = dprompts[1 if z < half else 0], z
        else:
            dprompt = dprompts[z * n_out // NZ]
            j = z % dprompt.shape[0]
        dprompt[j, :, :HEAD_DIMENSION] = k_grad[:PROMPT]
        dprompt[j, :, HEAD_DIMENSION:] = v_grad[:PROMPT]
        dnear[z, 0] = k_grad[PROMPT:]
        dnear[z, 1] = v_grad[PROMPT:]


def spread(keys, values, out, held, sems):
    copies = [
        pltpu.make_async_copy(ref, held.at[j], sems.at[j]) for j, ref in enumerate((keys, values))
    ]
    for copy in copies:
        copy.start()
    for j, copy in enumerate(copies):
        copy.wait()
        for h in range(HEADS):
            rows = held[j, :, h * HEAD_DIMENSION : (h + 1) * HEAD_DIMENSION]
            for z in range(NZ):
                out[z * HEADS + h, j] = rows


smem = pl.BlockSpec(memory_space=pltpu.SMEM)
vmem = pl.BlockSpec(memory_space=pltpu.VMEM)


def shaped(*shape):
    return jax.ShapeDtypeStruct(shape, jnp.bfloat16)


def call(body, outs, n_smem, n_vmem, n_scratch, flops, moved):
    return pl.pallas_call(
        body,
        out_shape=outs,
        in_specs=[smem] * n_smem + [vmem] * n_vmem,
        out_specs=[vmem] * len(outs),
        scratch_shapes=[pltpu.SMEM((NY * NZ,), jnp.int32)] * n_scratch,
        compiler_params=pltpu.CompilerParams(vmem_limit_bytes=24 * 1024 * 1024),
        cost_estimate=pl.CostEstimate(flops=flops, bytes_accessed=moved, transcendentals=0),
    )


def pack_call(turns, *args):
    n = len(turns)
    outs = [shaped(NZ, 2, GROUP * SPAN, HEAD_DIMENSION)] * n
    outs += [shaped(NZ, 2, SPAN, HEAD_DIMENSION)] * n
    outs += [jax.ShapeDtypeStruct((NZ, 1, GROUP * SPAN), jnp.float32)] * n
    got = call(functools.partial(pack, turns), outs, 4, 4, 3, 10**8, 2**10)(*args)
    return [got[i::n] for i in range(n)]


def unpack_call(turns, own_y, lengths, owners, wide, near, rows):
    outs = [shaped(rows, GROUP * HEAD_DIMENSION)] + [shaped(rows, HEAD_DIMENSION)] * 2
    body = functools.partial(unpack, turns)
    return call(body, outs, 3, 2 * len(turns), 2, 10**6, 2**10)(
        own_y, lengths, owners, *wide, *near
    )


def attend_call(packed, parts, n_out=1, early=()):
    whole = NZ if early else NZ // n_out
    outs = [shaped(NZ, HEAD_DIMENSION, GROUP * SPAN), shaped(NZ, 2, SPAN, HEAD_DIMENSION)]
    outs += [shaped(whole, PROMPT, 2 * HEAD_DIMENSION)] * n_out
    body = functools.partial(attend, len(parts), len(early), n_out)
    return call(body, outs, 0, 3 + len(parts) + len(early), 0, 10**6, 2**10)(
        *packed, *parts, *early
    )


def split_call(column):
    half = NZ // 2

    def split(column, low, high):
        low[...] = column[:half]
        high[...] = column[half:]

    outs = [shaped(half, *column.shape[1:])] * 2
    return call(split, outs, 0, 1, 0, 0, 2**20)(column)


def spread_call(keys, values):
    anywhere = pl.BlockSpec(memory_space=pl.ANY)
    return pl.pallas_call(
        spread,
        out_shape=shaped(NZ * HEADS, 2, keys.shape[0], HEAD_DIMENSION),
        in_specs=[anywhere] * 2,
        out_specs=vmem,
        scratch_shapes=[
            pltpu.VMEM((2,) + keys.shape, jnp.bfloat16),
            pltpu.SemaphoreType.DMA((2,)),
        ],
        compiler_params=pltpu.CompilerParams(vmem_limit_bytes=60 * 1024 * 1024),
    )(keys, values)


def along_y(turn):
    return [(z * NY + y, z * NY + (y + turn) % NY) for z in range(NZ) for y in range(NY)]


same_y_head = [[(z * NY + y) * HEADS + h for z in range(NZ) for h in range(HEADS)] for y in range(NY)]
same_y = [[z * NY + y for z in range(NZ)] for y in range(NY)]


def per_device(
    queries,
    response_keys,
    response_values,
    output_cotangent,
    prompt_key_rows,
    prompt_value_rows,
    resp_len,
    resp_owner,
    block_mask,
):
    part = prompt_key_rows.shape[0]
    half = NZ // 2
    column = lax.all_to_all(
        spread_call(prompt_key_rows, prompt_value_rows),
        ("dp", "head"),
        split_axis=0,
        concat_axis=0,
        axis_index_groups=same_y_head,
        tiled=True,
    ).reshape(NZ, HEADS, 2, part, HEAD_DIMENSION)
    turns = ((1, 3), (3, 1), (2, 2), (0, 0))
    own_y = lax.rem(lax.axis_index("dp"), NY).reshape(1).astype(jnp.int32)
    masks = block_mask.reshape(block_mask.shape[:2])
    scalars = (own_y, resp_len, resp_owner, masks)
    rows_of = (queries, output_cotangent, response_keys, response_values)
    first, second = pack_call(turns[:2], *scalars, *rows_of)
    far, own = pack_call(turns[2:], *scalars, *rows_of)
    column, first = lax.optimization_barrier((column, first))
    low, high = split_call(column)
    after_low = lax.ppermute(low, "dp", along_y(-1))
    before_high = lax.ppermute(high, "dp", along_y(1))
    after_high = lax.ppermute(high, "dp", along_y(-1))
    before_low = lax.ppermute(low, "dp", along_y(1))
    after_low, before_high, far = lax.optimization_barrier((after_low, before_high, far))
    across = [
        lax.ppermute(after_low, "dp", along_y(-1)),
        lax.ppermute(before_high, "dp", along_y(1)),
    ]
    made = [attend_call(first, [after_low, before_high], 2)]
    made.append(attend_call(second, [before_low, after_high], 2, made[0][2:]))
    made.append(attend_call(far, across))
    made.append(attend_call(own, [column]))
    dq = [a[0] for a in made]
    dnear = [a[1] for a in made]
    sums = [made[3][2]]
    for turn, part in zip((1, 3, 2), (*made[1][2:], made[2][2])):
        sums.append(lax.ppermute(part, "dp", along_y(turn)))
    dq, dk, dv = unpack_call(turns, own_y, resp_len, resp_owner, dq, dnear, queries.shape[0])
    summed = sum(a.astype(jnp.float32) for a in sums).astype(jnp.bfloat16)
    summed, dq, dk, dv = lax.optimization_barrier((summed, dq, dk, dv))
    shares = lax.all_to_all(
        summed, "dp", split_axis=0, concat_axis=0, axis_index_groups=same_y, tiled=True
    )
    whole = jnp.sum(shares.astype(jnp.float32), axis=0).astype(jnp.bfloat16)
    return (dq, dk, dv, whole[:, :HEAD_DIMENSION], whole[:, HEAD_DIMENSION:])


def solution(mesh):
    placed = (
        P("dp", "head"),
        P("dp", "head"),
        P("dp", "head"),
        P("dp", "head"),
        P(("dp", "head"), None),
        P(("dp", "head"), None),
        P("dp", None),
        P("dp", None),
        P("dp", None, None),
    )
    return jax.shard_map(
        per_device,
        mesh=mesh,
        in_specs=placed,
        out_specs=(
            P("dp", "head"),
            P("dp", "head"),
            P("dp", "head"),
            P("dp", "head"),
            P("dp", "head"),
        ),
        check_vma=False,
    )
```

```python
import functools
import math

import jax
import jax.numpy as jnp
from jax import lax
from jax.experimental import pallas as pl
from jax.experimental.pallas import tpu as pltpu
from jax.sharding import PartitionSpec as P

QUERY_HEADS = 64
KEY_VALUE_HEADS = 8
HEAD_DIMENSION = 128
GROUP = QUERY_HEADS // KEY_VALUE_HEADS
PROMPT = 128
SPAN = 32
WINDOW = 48
NY = 4
NZ = 8
HEADS = 8

far_below = -1e30
scale = 1.0 / math.sqrt(HEAD_DIMENSION)
exp2_scale = scale * math.log2(math.e)


def one_hot(shape, token_dim, offset, length):
    token = lax.broadcasted_iota(jnp.int32, shape, token_dim)
    place = lax.broadcasted_iota(jnp.int32, shape, 1 - token_dim)
    hit = (place == token + offset) & (token < length)
    return jnp.where(hit, 1.0, 0.0).astype(jnp.bfloat16)


def dot(a, b, dims=((1,), (0,))):
    return lax.dot_general(a, b, (dims, ((), ())), preferred_element_type=jnp.float32)


def locate(lengths, owners, masks, first_of, count_of, mask_of):
    def place(s, start):
        owner = owners[0, s]
        first_of[owner] = start
        count_of[owner] = lengths[0, s]
        if mask_of is not None:
            mask_of[owner] = masks[0, s]
        return start + lengths[0, s]

    lax.fori_loop(0, NY * NZ, place, jnp.int32(0))


def window_of(start, rows):
    base = pl.multiple_of(jnp.minimum((start // 16) * 16, rows - WINDOW), 16)
    return pl.ds(base, WINDOW), start - base


def pack(turns, own_y, lengths, owners, masks, query, cotangent, key, value, *refs):
    n = len(turns)
    wide, near, bias = refs[:n], refs[n : 2 * n], refs[2 * n : 3 * n]
    first_of, count_of, mask_of = refs[3 * n :]
    locate(lengths, owners, masks, first_of, count_of, mask_of)
    rows = query.shape[0]
    for turn, wide_ref, near_ref, bias_ref in zip(turns, wide, near, bias):
        y = lax.rem(own_y[0] + turn, NY)

        def one(z, carry):
            prompt = z * NY + y
            start = first_of[prompt]
            window, offset = window_of(start, rows)
            pick = one_hot((SPAN, WINDOW), 0, offset, count_of[prompt])
            for j, ref in enumerate((query, cotangent)):
                taken = dot(pick, ref[window, :]).astype(jnp.bfloat16)
                for h in range(GROUP):
                    wide_ref[z, j, h * SPAN : (h + 1) * SPAN, :] = taken[
                        :, h * HEAD_DIMENSION : (h + 1) * HEAD_DIMENSION
                    ]
            for j, ref in enumerate((key, value)):
                near_ref[z, j] = dot(pick, ref[window, :]).astype(jnp.bfloat16)
            hidden = jnp.where(mask_of[prompt] > 0, 0.0, far_below).astype(jnp.float32)
            bias_ref[z] = jnp.full(bias_ref.shape[1:], hidden, jnp.float32)
            return carry

        lax.fori_loop(0, NZ, one, 0, unroll=2)


def unpack(turns, own_y, lengths, owners, *refs):
    n = len(turns)
    wide, near = refs[:n], refs[n : 2 * n]
    dq, dk, dv, first_of, count_of = refs[2 * n :]
    locate(lengths, owners, None, first_of, count_of, None)
    rows = dq.shape[0]
    dq[...] = jnp.zeros_like(dq)
    dk[...] = jnp.zeros_like(dk)
    dv[...] = jnp.zeros_like(dv)
    for turn, wide_ref, near_ref in zip(turns, wide, near):
        y = lax.rem(own_y[0] + turn, NY)

        def one(i, carry):
            prompt = i * NY + y
            window, offset = window_of(first_of[prompt], rows)
            put = one_hot((WINDOW, SPAN), 1, offset, count_of[prompt])
            turned = wide_ref[i].T
            grads = jnp.concatenate(
                [turned[h * SPAN : (h + 1) * SPAN] for h in range(GROUP)], axis=1
            )
            dq[window, :] = dq[window, :] + dot(put, grads).astype(jnp.bfloat16)
            for j, ref in enumerate((dk, dv)):
                ref[window, :] = ref[window, :] + dot(put, near_ref[i, j]).astype(jnp.bfloat16)
            return carry

        lax.fori_loop(0, NZ, one, 0, unroll=2)


def attend(n_parts, wide, near, bias, *refs):
    parts = refs[:n_parts]
    dq, dnear, dprompt = refs[n_parts:]
    key_at = lax.broadcasted_iota(jnp.int32, (SPAN, GROUP * SPAN), 0)
    token_at = lax.broadcasted_iota(jnp.int32, (SPAN, GROUP * SPAN), 1) % SPAN
    near_bias = jnp.where(key_at <= token_at, 0.0, far_below)
    per_part = NZ // n_parts

    def rows_of(z, j):
        far = parts[z // per_part][z % per_part, :, j].reshape(PROMPT, HEAD_DIMENSION)
        return jnp.concatenate([far, near[z, j]])

    def products(z):
        return [dot(rows_of(z, j), wide[z, j], ((1,), (1,))) for j in range(2)]

    def soften(z, scores, dots):
        far, own = scores[:PROMPT], scores[PROMPT:] + near_bias
        hidden = bias[z]
        highest = jnp.maximum(
            jnp.max(far, axis=0, keepdims=True) + hidden, jnp.max(own, axis=0, keepdims=True)
        )
        weights = jnp.exp2(
            jnp.concatenate([far - (highest - hidden), own - highest], axis=0) * exp2_scale
        )
        inverse = 1.0 / jnp.sum(weights, axis=0, keepdims=True)
        delta = jnp.sum(weights * dots, axis=0, keepdims=True) * inverse
        probs = weights * inverse
        return (probs * (dots - delta)).astype(jnp.bfloat16), probs.astype(jnp.bfloat16)

    def gradients(z, slopes, probs):
        k_grad = (dot(slopes, wide[z, 0]) * scale).astype(jnp.bfloat16)
        v_grad = dot(probs, wide[z, 1]).astype(jnp.bfloat16)
        dq[z] = (dot(rows_of(z, 0), slopes, ((0,), (0,))) * scale).astype(jnp.bfloat16)
        dprompt[z, :, :HEAD_DIMENSION] = k_grad[:PROMPT]
        dprompt[z, :, HEAD_DIMENSION:] = v_grad[:PROMPT]
        dnear[z, 0] = k_grad[PROMPT:]
        dnear[z, 1] = v_grad[PROMPT:]

    ahead, behind = products(0), None
    for z in range(NZ):
        held = ahead
        if z + 1 < NZ:
            ahead = products(z + 1)
        if behind is not None:
            gradients(z - 1, *behind)
        behind = soften(z, *held)
    gradients(NZ - 1, *behind)


def spread(keys, values, out, held, sems):
    copies = [
        pltpu.make_async_copy(ref, held.at[j], sems.at[j]) for j, ref in enumerate((keys, values))
    ]
    for copy in copies:
        copy.start()
    for j, copy in enumerate(copies):
        copy.wait()
        for h in range(HEADS):
            rows = held[j, :, h * HEAD_DIMENSION : (h + 1) * HEAD_DIMENSION]
            for z in range(NZ):
                out[z * HEADS + h, j] = rows


smem = pl.BlockSpec(memory_space=pltpu.SMEM)
vmem = pl.BlockSpec(memory_space=pltpu.VMEM)


def shaped(*shape):
    return jax.ShapeDtypeStruct(shape, jnp.bfloat16)


def call(body, outs, n_smem, n_vmem, n_scratch, flops, moved):
    return pl.pallas_call(
        body,
        out_shape=outs,
        in_specs=[smem] * n_smem + [vmem] * n_vmem,
        out_specs=[vmem] * len(outs),
        scratch_shapes=[pltpu.SMEM((NY * NZ,), jnp.int32)] * n_scratch,
        compiler_params=pltpu.CompilerParams(vmem_limit_bytes=24 * 1024 * 1024),
        cost_estimate=pl.CostEstimate(flops=flops, bytes_accessed=moved, transcendentals=0),
    )


def pack_call(turns, *args):
    n = len(turns)
    outs = [shaped(NZ, 2, GROUP * SPAN, HEAD_DIMENSION)] * n
    outs += [shaped(NZ, 2, SPAN, HEAD_DIMENSION)] * n
    outs += [jax.ShapeDtypeStruct((NZ, 1, GROUP * SPAN), jnp.float32)] * n
    got = call(functools.partial(pack, turns), outs, 4, 4, 3, 10**8, 2**10)(*args)
    return [got[i::n] for i in range(n)]


def unpack_call(turns, own_y, lengths, owners, wide, near, rows):
    outs = [shaped(rows, GROUP * HEAD_DIMENSION)] + [shaped(rows, HEAD_DIMENSION)] * 2
    body = functools.partial(unpack, turns)
    return call(body, outs, 3, 2 * len(turns), 2, 10**6, 2**10)(
        own_y, lengths, owners, *wide, *near
    )


def attend_call(packed, parts):
    outs = [
        shaped(NZ, HEAD_DIMENSION, GROUP * SPAN),
        shaped(NZ, 2, SPAN, HEAD_DIMENSION),
        shaped(NZ, PROMPT, 2 * HEAD_DIMENSION),
    ]
    body = functools.partial(attend, len(parts))
    return call(body, outs, 0, 3 + len(parts), 0, 10**6, 2**10)(*packed, *parts)


def split_call(column):
    half = NZ // 2

    def split(column, low, high):
        low[...] = column[:half]
        high[...] = column[half:]

    outs = [shaped(half, *column.shape[1:])] * 2
    return call(split, outs, 0, 1, 0, 0, 2**20)(column)


def spread_call(keys, values):
    anywhere = pl.BlockSpec(memory_space=pl.ANY)
    return pl.pallas_call(
        spread,
        out_shape=shaped(NZ * HEADS, 2, keys.shape[0], HEAD_DIMENSION),
        in_specs=[anywhere] * 2,
        out_specs=vmem,
        scratch_shapes=[
            pltpu.VMEM((2,) + keys.shape, jnp.bfloat16),
            pltpu.SemaphoreType.DMA((2,)),
        ],
        compiler_params=pltpu.CompilerParams(vmem_limit_bytes=60 * 1024 * 1024),
    )(keys, values)


def along_y(turn):
    return [(z * NY + y, z * NY + (y + turn) % NY) for z in range(NZ) for y in range(NY)]


same_y_head = [[(z * NY + y) * HEADS + h for z in range(NZ) for h in range(HEADS)] for y in range(NY)]
same_y = [[z * NY + y for z in range(NZ)] for y in range(NY)]


def per_device(
    queries,
    response_keys,
    response_values,
    output_cotangent,
    prompt_key_rows,
    prompt_value_rows,
    resp_len,
    resp_owner,
    block_mask,
):
    part = prompt_key_rows.shape[0]
    half = NZ // 2
    column = lax.all_to_all(
        spread_call(prompt_key_rows, prompt_value_rows),
        ("dp", "head"),
        split_axis=0,
        concat_axis=0,
        axis_index_groups=same_y_head,
        tiled=True,
    ).reshape(NZ, HEADS, 2, part, HEAD_DIMENSION)
    own_y = lax.rem(lax.axis_index("dp"), NY).reshape(1).astype(jnp.int32)
    masks = block_mask.reshape(block_mask.shape[:2])
    scalars = (own_y, resp_len, resp_owner, masks)
    rows_of = (queries, output_cotangent, response_keys, response_values)
    next_one, last_one = pack_call((1, 3), *scalars, *rows_of)
    far, own = pack_call((2, 0), *scalars, *rows_of)
    column, next_one = lax.optimization_barrier((column, next_one))
    low, high = split_call(column)
    after_low = lax.ppermute(low, "dp", along_y(-1))
    before_high = lax.ppermute(high, "dp", along_y(1))
    across = [
        lax.ppermute(after_low, "dp", along_y(-1)),
        lax.ppermute(before_high, "dp", along_y(1)),
    ]
    after = [after_low, lax.ppermute(high, "dp", along_y(-1))]
    before = [lax.ppermute(low, "dp", along_y(1)), before_high]
    after, before, far = lax.optimization_barrier((after, before, far))
    dq, dnear, sums = [], [], []
    order = (1, 2, 3, 0)
    for turn, packed, prompts in (
        (1, next_one, after),
        (2, far, across),
        (3, last_one, before),
        (0, own, [column]),
    ):
        q_part, near_part, prompt_part = attend_call(packed, prompts)
        dq.append(q_part)
        dnear.append(near_part)
        sums.append(lax.ppermute(prompt_part, "dp", along_y(turn)) if turn else prompt_part)
    dq, dk, dv = unpack_call(
        order, own_y, resp_len, resp_owner, dq, dnear, queries.shape[0]
    )
    summed = sum(a.astype(jnp.float32) for a in sums).astype(jnp.bfloat16)
    summed, dq, dk, dv = lax.optimization_barrier((summed, dq, dk, dv))
    shares = lax.all_to_all(
        summed, "dp", split_axis=0, concat_axis=0, axis_index_groups=same_y, tiled=True
    )
    whole = jnp.sum(shares.astype(jnp.float32), axis=0).astype(jnp.bfloat16)
    return (dq, dk, dv, whole[:, :HEAD_DIMENSION], whole[:, HEAD_DIMENSION:])


def solution(mesh):
    placed = (
        P("dp", "head"),
        P("dp", "head"),
        P("dp", "head"),
        P("dp", "head"),
        P(("dp", "head"), None),
        P(("dp", "head"), None),
        P("dp", None),
        P("dp", None),
        P("dp", None, None),
    )
    return jax.shard_map(
        per_device,
        mesh=mesh,
        in_specs=placed,
        out_specs=(
            P("dp", "head"),
            P("dp", "head"),
            P("dp", "head"),
            P("dp", "head"),
            P("dp", "head"),
        ),
        check_vma=False,
    )
```
